128 devices in a mesh: lon: 16 (over y, z_lo, core), lat: 8 (over z_hi, x).
Axes of the slice: x: 4, y: 4, z: 4 (z_hi: 2, z_lo: 2; z = z_hi * 2 + z_lo), core: 2. Of those that a mesh axis runs over, the one named last changes fastest.
Arguments:
- tokens: bfloat16 [288, 384, 4, 512], P('lat', 'lon'), may hold values from -6 to 6
- norm1_gain: float32 [512], replicated, may hold values from 0.1 to 1.9
- norm1_bias: float32 [512], replicated, may hold values from -3 to 3
- qkv_weight: bfloat16 [512, 1536], replicated
- rel_bias: float32 [8, 759], replicated, may hold values from -4 to 4
- key_mask: int32 [288, 384], replicated, may hold values from 0 to 1, as said below
- proj_weight: bfloat16 [512, 512], replicated, may hold values from -0.25 to 0.25
- norm2_gain: float32 [512], replicated, may hold values from 0.1 to 1.9
- norm2_bias: float32 [512], replicated, may hold values from -3 to 3
- fc1_weight: bfloat16 [512, 2048], replicated, may hold values from -0.25 to 0.25
- fc2_weight: bfloat16 [2048, 512], replicated, may hold values from -0.125 to 0.125
Outputs:
- block_out: bfloat16 [288, 384, 4, 512], P('lat', 'lon')
The draws below stay inside these ranges and needn't reach their ends.
Inputs may be any that keep to these rules, and one draw needn't show every extreme that they name: `key_mask`: whole rows next to each pole are 0, and scattered cells elsewhere.
All inputs are finite; a program needn't handle non-finite values.
Results may differ from the reference program's by a relative error of at most 0.0059.
Values may be sent and summed in bfloat16 or wider, within the bound.
No kernel may reach another device: no remote copies, remote signals or barrier semaphores. Data moves between devices by JAX's collectives and lax.ppermute only.
A program may use at most 192 MiB of HBM per device.

```python
import jax
import jax.numpy as jnp
import numpy as np
from jax import lax

C = 512
HEADS = 8
FF = 2048
WLEV = 2
WLAT = 6
WLON = 12
LEV = 4
SLEV = 1
SLAT = 3
SLON = 6
HEAD_DIM = 64
TABLE = 759
NLAT = 288
NLON = 384


def draw_qkv_weight(key, part):
    key = jax.random.fold_in(key, 11)
    base = jnp.clip(jax.random.normal(key, (C, 3 * C), jnp.float32), -4.0, 4.0) * C ** (-0.5)
    return base.astype(jnp.bfloat16)


def draw_key_mask(key, part):
    key = jax.random.fold_in(key, 23)
    sub_keys = jax.random.split(key, 3)
    north_rows = jax.random.randint(sub_keys[0], (), 1, 3)
    south_rows = jax.random.randint(sub_keys[1], (), 1, 3)
    holes_draw = jax.random.randint(sub_keys[2], (NLAT, NLON), 0, 8)
    row_index = jnp.arange(NLAT, dtype=jnp.int32)[:, None]
    keep_cell = (row_index >= north_rows) & (row_index < NLAT - south_rows) & (holes_draw > 0)
    return keep_cell.astype(jnp.int32)


def levels(own_key, dims, cuts, low, largest):
    def one(dim, shards_of):
        draws = jax.random.uniform(jax.random.fold_in(jax.random.fold_in(own_key, 6), dim), (shards_of,), jnp.float32, low / len(cuts), largest / len(cuts))
        return jnp.repeat(jnp.exp(draws), dims[dim] // shards_of).reshape((-1,) + (1,) * (len(dims) - dim - 1))

    loudness = one(*cuts[0])
    for cut in cuts[1:]:
        loudness = loudness * one(*cut)
    return loudness


def noise(stream_key, extent, scale, most, shards=(), kind=jnp.bfloat16):
    factor_of = levels(stream_key, extent, shards, -0.22, 0.18) if shards else 1.0
    values = jax.random.normal(stream_key, extent, jnp.float32) * scale * factor_of
    return jnp.minimum(jnp.maximum(values, -most), most).astype(kind)


def setup_inputs(seed: int = 0) -> dict:
    key_of = jax.random.split(jax.random.key(seed), 12)
    return {
        "tokens": noise(key_of[0], (NLAT, NLON, LEV, C), 1.0, 6.0, ((0, 8), (1, 16))),
        "norm1_gain": jnp.clip(1.0 + 0.18 * jax.random.normal(key_of[1], (C,), jnp.float32), 0.1, 1.9),
        "norm1_bias": noise(key_of[2], (C,), 0.5, 3.0, (), jnp.float32),
        "qkv_weight": draw_qkv_weight(jax.random.fold_in(key_of[11], 71), 0),
        "rel_bias": noise(key_of[4], (HEADS, TABLE), 1.0, 4.0, (), jnp.float32),
        "key_mask": draw_key_mask(jax.random.fold_in(key_of[11], 71), 0),
        "proj_weight": noise(key_of[6], (C, C), C ** -0.5, 0.25),
        "norm2_gain": jnp.clip(1.0 + 0.18 * jax.random.normal(key_of[7], (C,), jnp.float32), 0.1, 1.9),
        "norm2_bias": noise(key_of[8], (C,), 0.5, 3.0, (), jnp.float32),
        "fc1_weight": noise(key_of[9], (C, FF), C ** -0.5, 0.25),
        "fc2_weight": noise(key_of[10], (FF, C), FF ** -0.5, 0.125),
    }


epsilon = 1e-05

def window_index():
    lat_grid, lon_grid, lev_grid = np.meshgrid(np.arange(WLAT), np.arange(WLON), np.arange(WLEV), indexing='ij')
    lat_pos = lat_grid.reshape(-1)
    lon_pos = lon_grid.reshape(-1)
    lev_pos = lev_grid.reshape(-1)
    lon_span = 2 * WLON - 1
    lev_span = 2 * WLEV - 1
    combined = (lat_pos[:, None] - lat_pos[None, :] + WLAT - 1) * lon_span * lev_span
    combined = combined + (lon_pos[:, None] - lon_pos[None, :] + WLON - 1) * lev_span
    combined = combined + (lev_pos[:, None] - lev_pos[None, :] + WLEV - 1)
    return combined.astype(np.int32)

def layer_norm(values, gain, offset):
    values = values.astype(jnp.float32)
    average = lax.optimization_barrier(jnp.mean(values, axis=-1, keepdims=True))
    centred = values - average
    spread = lax.optimization_barrier(jnp.mean(centred * centred, axis=-1, keepdims=True))
    return centred * lax.rsqrt(spread + epsilon) * gain + offset

def to_windows(array, height, width):
    features = array.shape[-1]
    shaped = array.reshape(height // WLAT, WLAT, width // WLON, WLON, LEV // WLEV, WLEV, features)
    return shaped.transpose(0, 2, 4, 1, 3, 5, 6).reshape(-1, WLAT * WLON * WLEV, features)

def from_windows(windows, height, width):
    features = windows.shape[-1]
    shaped = windows.reshape(height // WLAT, width // WLON, LEV // WLEV, WLAT, WLON, WLEV, features)
    return shaped.transpose(0, 3, 1, 4, 2, 5, 6).reshape(height, width, LEV, features)

def window_context(triples, valid_rows, region_rows, bias_full):
    width = triples.shape[1]
    windows = to_windows(triples, WLAT, width)
    window_count = windows.shape[0]
    window_size = windows.shape[1]
    query_heads = windows[:, :, :C].astype(jnp.float32).reshape(window_count, window_size, HEADS, HEAD_DIM)
    key_heads = windows[:, :, C:2 * C].astype(jnp.float32).reshape(window_count, window_size, HEADS, HEAD_DIM)
    value_heads = windows[:, :, 2 * C:].astype(jnp.float32).reshape(window_count, window_size, HEADS, HEAD_DIM)
    level_region = ((jnp.arange(LEV) + SLEV) % LEV == 0).astype(jnp.int32)
    region = jnp.broadcast_to(region_rows[:, None, None] * 2 + level_region[None, None, :], (WLAT, width, LEV))
    region = to_windows(region[..., None], WLAT, width)[..., 0]
    valid_keys = jnp.broadcast_to(valid_rows[:, :, None], (WLAT, width, LEV))
    valid_keys = to_windows(valid_keys[..., None], WLAT, width)[..., 0]
    scores = jnp.einsum('aqhd,akhd->ahqk', query_heads, key_heads, precision=lax.Precision.HIGHEST)
    scores = scores * HEAD_DIM ** (-0.5) + bias_full[None]
    allowed = (region[:, :, None] == region[:, None, :]) & ((valid_keys[:, None, :] > 0) | jnp.eye(window_size, dtype=jnp.bool_)[None])
    scores = jnp.where(allowed[:, None], scores, -jnp.inf)
    row_max = lax.optimization_barrier(jnp.max(scores, axis=-1, keepdims=True))
    powered = jnp.exp(scores - row_max)
    weights_bf = (powered / lax.optimization_barrier(jnp.sum(powered, axis=-1, keepdims=True))).astype(jnp.bfloat16)
    context = jnp.einsum('ahqk,akhd->aqhd', weights_bf.astype(jnp.float32), value_heads, precision=lax.Precision.HIGHEST)
    context = context.reshape(window_count, window_size, C).astype(jnp.bfloat16)
    return from_windows(context, WLAT, width)

def attend_rows(row_block, qkv_weight, proj_weight, bias_full):
    normed_rows, valid_rows, region_rows = row_block
    width = normed_rows.shape[1]
    triples = jnp.dot(normed_rows.reshape(-1, C), qkv_weight, preferred_element_type=jnp.float32).astype(jnp.bfloat16)
    triples = triples.reshape(WLAT, width, LEV, 3 * C)
    context = window_context(triples, valid_rows, region_rows, bias_full)
    moved = jnp.dot(context.reshape(-1, C), proj_weight, preferred_element_type=jnp.float32).astype(jnp.bfloat16)
    return moved.reshape(WLAT, width, LEV, C)

def feed_rows(row_block, norm2_gain, norm2_bias, fc1_weight, fc2_weight):
    token_rows, attended_rows = row_block
    middle = token_rows.astype(jnp.float32) + attended_rows.astype(jnp.float32)
    normed2 = layer_norm(middle, norm2_gain, norm2_bias).astype(jnp.bfloat16).reshape(-1, C)
    hidden = jax.nn.gelu(jnp.dot(normed2, fc1_weight, preferred_element_type=jnp.float32), approximate=False).astype(jnp.bfloat16)
    result = middle.reshape(-1, C) + jnp.dot(hidden, fc2_weight, preferred_element_type=jnp.float32)
    return result.astype(jnp.bfloat16).reshape(token_rows.shape)

def reference(tokens, norm1_gain, norm1_bias, qkv_weight, rel_bias, key_mask, proj_weight, norm2_gain, norm2_bias, fc1_weight, fc2_weight):
    normed = layer_norm(tokens, norm1_gain, norm1_bias).astype(jnp.bfloat16)
    shifted = jnp.roll(normed, (-SLAT, -SLON, -SLEV), axis=(0, 1, 2))
    valid_keys = jnp.roll(key_mask, (-SLAT, -SLON), axis=(0, 1))
    region_rows = ((jnp.arange(NLAT) + SLAT) % NLAT < SLAT).astype(jnp.int32)
    bias_full = rel_bias[:, window_index()]
    blocks = NLAT // WLAT
    stacked = (shifted.reshape(blocks, WLAT, NLON, LEV, C), valid_keys.reshape(blocks, WLAT, NLON), region_rows.reshape(blocks, WLAT))
    moved = lax.map(lambda row_block: attend_rows(row_block, qkv_weight, proj_weight, bias_full), stacked)
    attended = jnp.roll(moved.reshape(NLAT, NLON, LEV, C), (SLAT, SLON, SLEV), axis=(0, 1, 2))
    paired = (tokens.reshape(blocks, WLAT, NLON, LEV, C), attended.reshape(blocks, WLAT, NLON, LEV, C))
    result = lax.map(lambda row_block: feed_rows(row_block, norm2_gain, norm2_bias, fc1_weight, fc2_weight), paired)
    return result.reshape(NLAT, NLON, LEV, C)
```

```python
import functools
import math

import jax
import jax.numpy as jnp
import numpy as np
from jax import lax
from jax.experimental import pallas as pl
from jax.experimental.pallas import tpu as pltpu
from jax.sharding import PartitionSpec as P

C = 512
FF = 2048
HEADS = 8
HEAD_DIM = 64
WLEV = 2
WLAT = 6
WLON = 12
LEV = 4
SLAT = 3
SLON = 6
WIN = WLAT * WLON * WLEV
HALF = WIN // 2
QUART = WIN // 4
EPS = 1e-5
LOG2E = math.log2(math.e)
NEG = -jnp.inf
BF = jnp.bfloat16
F32 = jnp.float32
PAIRS = ((1, 2), (3, 0))
VMEM_LIMIT = 56 * 1024 * 1024
ERF = (0.7978281359956358, 0.036468790964347284, -0.00012486163691975404,
       -3.0581006276508824e-05, 1.1190821930105387e-06)


def order_columns():
    first = [(p, 6 * h + q, r) for h in range(2) for r in range(2) for p in range(6) for q in range(6)]
    second = [(3 * h + p, q, r) for h in range(2) for r in range(2) for p in range(3) for q in range(12)]
    return first, second


def lane_pqr(u, which):
    half, r, cell = u // HALF, (u // QUART) % 2, u % QUART
    if which == 0:
        return cell // 6, 6 * half + cell % 6, r
    return 3 * half + cell // 12, cell % 12, r


def prep_kernel(place_ref, table_ref, mask_ref, bias1_ref, bias2_ref, valid_ref, rows_ref, *, shape):
    lat, lon, lats = place_ref[0], place_ref[1], shape[0] // shape[2]
    table = table_ref[...] * LOG2E
    out_refs = (bias1_ref, bias2_ref)
    for which, order in enumerate(order_columns()):
        for t, (p, q, r) in enumerate(order):
            start = p * 69 + q * 3 + r
            rows_ref[8 * t : 8 * t + 8, :] = table[:, start : start + 384]
        rows = rows_ref[...]
        high = rows.astype(BF)
        low = (rows - high.astype(F32)).astype(BF)
        k = lax.broadcasted_iota(jnp.int32, (384, WIN), 0)
        p, q, r = lane_pqr(lax.broadcasted_iota(jnp.int32, (384, WIN), 1), which)
        pick = (k == 379 - (p * 69 + q * 3 + r)).astype(F32).astype(BF)
        full = jnp.dot(high, pick, preferred_element_type=F32) + jnp.dot(low, pick, preferred_element_type=F32)
        full = jnp.transpose(full.reshape(WIN, HEADS, WIN), (1, 0, 2))
        t = lax.broadcasted_iota(jnp.int32, (WIN, WIN), 0)
        u = lax.broadcasted_iota(jnp.int32, (WIN, WIN), 1)
        same = (t // QUART) % 2 == (u // QUART) % 2
        for h in range(HEADS):
            out_refs[which][h, 0] = full[h]
            out_refs[which][h, 1] = jnp.where(same, full[h], NEG)
    nlat, nlon, tile_rows, tile_cols = shape
    row = lax.broadcasted_iota(jnp.int32, (48, nlat), 0)
    col = lax.broadcasted_iota(jnp.int32, (48, nlat), 1)
    want = lax.rem(lat * tile_rows - SLAT + row + nlat, nlat)
    pick_rows = (want == col).astype(F32).astype(BF)
    mask = (mask_ref[...] > 0).astype(F32).astype(BF)
    picked = jnp.dot(pick_rows, mask, preferred_element_type=F32).astype(BF)
    for which in range(2):
        row = lax.broadcasted_iota(jnp.int32, (nlon, 3 * WIN), 0)
        lane = lax.broadcasted_iota(jnp.int32, (nlon, 3 * WIN), 1)
        _, q, _ = lane_pqr(lane % WIN, which)
        want = lax.rem(lon * tile_cols - SLON + 12 * (lane // WIN) + q + nlon, nlon)
        pick_cols = (want == row).astype(F32).astype(BF)
        spread = jnp.dot(picked, pick_cols, preferred_element_type=F32)
        row = lax.broadcasted_iota(jnp.int32, (48, 3 * WIN), 0)
        lane = lax.broadcasted_iota(jnp.int32, (48, 3 * WIN), 1)
        p, _, _ = lane_pqr(lane % WIN, which)
        lane1 = lax.broadcasted_iota(jnp.int32, (1, 3 * WIN), 1)
        for window in (range(1, 6) if which == 0 else (0, 6)):
            value = jnp.sum(jnp.where(row == 6 * window + p, spread, 0.0), axis=0, keepdims=True)
            ok = value > 0.5
            if window == 0:
                ok = ok & ((lat > 0) | (lane1 % WIN >= HALF))
            if window == 6:
                ok = ok & ((lat < lats - 1) | (lane1 % WIN < HALF))
            value = jnp.where(ok, 0.0, NEG)
            for k in range(3):
                valid_ref[3 * window + k] = value[:, k * WIN : (k + 1) * WIN]


def layer_norm(values, gain, offset):
    average = jnp.mean(values, axis=-1, keepdims=True)
    centred = values - average
    spread = jnp.mean(centred * centred, axis=-1, keepdims=True)
    return centred * lax.rsqrt(spread + EPS) * gain + offset


def by_level(block):
    cells = block.astype(F32).reshape(QUART, LEV, C)
    return jnp.transpose(cells, (1, 0, 2))


def from_level(rows, shape):
    return jnp.transpose(rows, (1, 0, 2)).reshape(shape).astype(BF)


def attend(q, k, v, bias_of, block_mask):
    n = q.shape[0]
    head_of = lax.broadcasted_iota(jnp.int32, (1, 256), 1) // HEAD_DIM
    parts = []
    for g in range(2):
        lanes = slice(256 * g, 256 * g + 256)
        qg = q[:, lanes]
        stacked = jnp.concatenate([jnp.where(head_of == j, qg, 0.0) for j in range(4)], axis=0).astype(BF)
        scores = lax.dot_general(stacked, k[:, lanes], (((1,), (1,)), ((), ())), preferred_element_type=F32)
        probs, scale = [], []
        for j in range(4):
            s = scores[j * n : (j + 1) * n] + (bias_of(4 * g + j) + block_mask)
            powered = jnp.exp2(s - jnp.max(s, axis=-1, keepdims=True))
            scale.append(1.0 / jnp.sum(powered, axis=-1, keepdims=True))
            probs.append(powered)
        probs = jnp.concatenate(probs, axis=0).astype(BF)
        out = jnp.dot(probs, v[:, lanes], preferred_element_type=F32)
        context = out[:n] * scale[0]
        for j in range(1, 4):
            context = jnp.where(head_of == j, out[j * n : (j + 1) * n] * scale[j], context)
        parts.append(context)
    return jnp.concatenate(parts, axis=1)


def feed(middle, gain, offset, fc1_ref, fc2_ref):
    normed = layer_norm(middle, gain, offset).astype(BF)
    total = None
    for j in range(4):
        v = jnp.dot(normed, fc1_ref[:, 512 * j : 512 * j + 512], preferred_element_type=F32)
        y = v * v
        poly = ERF[4] * y + ERF[3]
        for c in ERF[2::-1]:
            poly = poly * y + c
        hidden = (v + v * jnp.tanh(v * poly)).astype(BF)
        part = jnp.dot(hidden, fc2_ref[512 * j : 512 * j + 512, :], preferred_element_type=F32)
        total = part if total is None else total + part
    return middle + 0.5 * total


def key_block_mask(valid, first, n):
    t = lax.broadcasted_iota(jnp.int32, (n, WIN), 0) + first
    u = lax.broadcasted_iota(jnp.int32, (n, WIN), 1)
    return jnp.where(t == u, 0.0, jnp.broadcast_to(valid, (n, WIN)))


def inner_kernel(tok_ref, g1_ref, b1_ref, qkv_ref, bias_ref, valid_ref, proj_ref, g2_ref, b2_ref,
                 fc1_ref, fc2_ref, out_ref, xs_ref, q_ref, kv_ref, ctx_ref):
    i = pl.program_id(0)
    x = tok_ref[...]
    for h in range(2):
        levels = by_level(x[:, 6 * h : 6 * h + 6])
        for pair in range(2):
            for r in range(2):
                at = WIN * pair + HALF * h + QUART * r
                xs_ref[at : at + QUART, :] = levels[PAIRS[pair][r]]
    normed = layer_norm(xs_ref[...], g1_ref[...], b1_ref[...]).astype(BF)
    q_ref[...] = jnp.dot(normed, qkv_ref[:, :C], preferred_element_type=F32) * (HEAD_DIM ** -0.5 * LOG2E)
    kv_ref[...] = jnp.dot(normed, qkv_ref[:, C:], preferred_element_type=F32).astype(BF)
    block_mask = key_block_mask(valid_ref[3 * (i + 1) + 1], 0, WIN)
    for pair in range(2):
        rows = slice(WIN * pair, WIN * pair + WIN)
        context = attend(q_ref[rows, :], kv_ref[rows, :C], kv_ref[rows, C:],
                         lambda h: bias_ref[h, pair], block_mask)
        ctx_ref[rows, :] = context.astype(BF)
    moved = jnp.dot(ctx_ref[...], proj_ref[...], preferred_element_type=F32).astype(BF)
    middle = xs_ref[...] + moved.astype(F32)
    xs_ref[...] = feed(middle, g2_ref[...], b2_ref[...], fc1_ref, fc2_ref)
    for h in range(2):
        levels = [None] * LEV
        for pair in range(2):
            for r in range(2):
                at = WIN * pair + HALF * h + QUART * r
                levels[PAIRS[pair][r]] = xs_ref[at : at + QUART, :]
        out_ref[:, 6 * h : 6 * h + 6] = from_level(jnp.stack(levels), (6, 6, LEV, C))


def half_windows(windows, refs, bias_ref, results):
    g1, b1, qkv_ref, proj_ref, g2, b2, fc1_ref, fc2_ref, xs_ref, q_ref, kv_ref, own_ref = refs
    count = len(windows)
    total = 2 * WIN * count
    for w, (own, halo, own_first, _) in enumerate(windows):
        for block, here in ((own, own_first), (halo, not own_first)):
            levels = by_level(block)
            for pair in range(2):
                for r in range(2):
                    at = 2 * WIN * w + WIN * pair + (0 if here else HALF) + QUART * r
                    xs_ref[at : at + QUART, :] = levels[PAIRS[pair][r]]

    def own_rows(array):
        pieces = []
        for w in range(count):
            for pair in range(2):
                at = 2 * WIN * w + WIN * pair + (0 if windows[w][2] else HALF)
                pieces.append(array[at : at + HALF])
        return jnp.concatenate(pieces, axis=0)

    normed = layer_norm(xs_ref[:total, :], g1, b1)
    q_ref[: total // 2, :] = jnp.dot(own_rows(normed).astype(BF), qkv_ref[:, :C], preferred_element_type=F32) * (
        HEAD_DIM ** -0.5 * LOG2E)
    kv_ref[:total, :] = jnp.dot(normed.astype(BF), qkv_ref[:, C:], preferred_element_type=F32).astype(BF)
    contexts = []
    for w in range(count):
        first = 0 if windows[w][2] else HALF
        block_mask = key_block_mask(windows[w][3], first, HALF)
        for pair in range(2):
            at = 2 * WIN * w + WIN * pair
            mine = HALF * (2 * w + pair)
            contexts.append(attend(q_ref[mine : mine + HALF, :], kv_ref[at : at + WIN, :C], kv_ref[at : at + WIN, C:],
                                   lambda h: bias_ref[h, pair, first : first + HALF, :], block_mask))
    context = jnp.concatenate(contexts, axis=0).astype(BF)
    moved = jnp.dot(context, proj_ref[...], preferred_element_type=F32).astype(BF)
    middle = own_rows(xs_ref) + moved.astype(F32)
    own_ref[: total // 2, :] = feed(middle, g2, b2, fc1_ref, fc2_ref)
    for w in range(count):
        levels = [None] * LEV
        for pair in range(2):
            for r in range(2):
                at = HALF * (2 * w + pair) + QUART * r
                levels[PAIRS[pair][r]] = own_ref[at : at + QUART, :]
        results(w, jnp.stack(levels))


def edge_kernel(part_ref, tok_ref, west_ref, east_ref, north_ref, south_ref, nw_ref, ne_ref, sw_ref, se_ref,
                g1_ref, b1_ref, qkv_ref, bias1_ref, bias2_ref, valid_ref, proj_ref, g2_ref, b2_ref,
                fc1_ref, fc2_ref, out_ref, xs_ref, q_ref, kv_ref, own_ref, sides_ref, strip_ref, side_sem, strip_sem):
    del part_ref
    rows, cols = tok_ref.shape[:2]
    refs = (g1_ref[...], b1_ref[...], qkv_ref, proj_ref, g2_ref[...], b2_ref[...], fc1_ref, fc2_ref,
            xs_ref, q_ref, kv_ref, own_ref)

    def side_copies(i, slot):
        at = pl.ds(SLAT + WLAT * i, WLAT)
        return [pltpu.make_async_copy(sides_ref.at[slot, side], out_ref.at[at, pl.ds(where, SLON)],
                                      side_sem.at[slot, side])
                for side, where in ((0, 0), (1, cols - SLON))]

    def sides(i, carry):
        slot = lax.rem(i, 2)
        at = pl.ds(SLAT + WLAT * i, WLAT)
        windows = (
            (tok_ref[at, 0:SLON], west_ref[at], False, valid_ref[3 * (i + 1)]),
            (tok_ref[at, cols - SLON : cols], east_ref[at], True, valid_ref[3 * (i + 1) + 2]),
        )

        @pl.when(i >= 2)
        def _():
            for copy in side_copies(i - 2, slot):
                copy.wait()

        def results(w, levels):
            sides_ref[slot, w] = from_level(levels, (WLAT, SLON, LEV, C))

        half_windows(windows, refs, bias1_ref, results)
        for copy in side_copies(i, slot):
            copy.start()
        return carry

    steps = (rows - WLAT) // WLAT
    lax.fori_loop(0, steps, sides, 0)

    copies = []
    for which in range(2):
        if which == 0:
            own_rows, own_first, mid, left, right = slice(0, SLAT), False, north_ref, nw_ref, ne_ref
        else:
            own_rows, own_first, mid, left, right = slice(rows - SLAT, rows), True, south_ref, sw_ref, se_ref
        own = jnp.concatenate([west_ref[own_rows], tok_ref[own_rows], east_ref[own_rows]], axis=1)
        halo = jnp.concatenate([left[...], mid[...], right[...]], axis=1)
        windows = tuple(
            (own[:, WLON * k : WLON * k + WLON], halo[:, WLON * k : WLON * k + WLON], own_first,
             valid_ref[18 * which + k]) for k in range(3))

        def results(w, levels):
            block = from_level(levels, (SLAT, WLON, LEV, C))
            if w == 0:
                strip_ref[which, :, 0:SLON] = block[:, SLON:]
            elif w == 1:
                strip_ref[which, :, SLON : SLON + WLON] = block
            else:
                strip_ref[which, :, SLON + WLON :] = block[:, :SLON]

        half_windows(windows, refs, bias2_ref, results)
        copy = pltpu.make_async_copy(strip_ref.at[which], out_ref.at[own_rows], strip_sem.at[which])
        copy.start()
        copies.append(copy)
    for i in (steps - 2, steps - 1):
        for copy in side_copies(i, i % 2):
            copy.wait()
    for copy in copies:
        copy.wait()


def passed_along(block, axes, distance):
    sizes = [lax.axis_size(a) for a in axes]
    route = []
    for i in np.ndindex(*sizes):
        j = tuple((a - d) % s for a, d, s in zip(i, distance, sizes))
        route.append((int(np.ravel_multi_index(j, sizes)), int(np.ravel_multi_index(i, sizes))))
    return lax.ppermute(block, axes if len(axes) > 1 else axes[0], route)


def per_device(tokens, norm1_gain, norm1_bias, qkv_weight, rel_bias, key_mask, proj_weight,
               norm2_gain, norm2_bias, fc1_weight, fc2_weight):
    rows, cols = tokens.shape[:2]
    west = passed_along(tokens[:, cols - SLON :], ("lon",), (1,))
    east = passed_along(tokens[:, :SLON], ("lon",), (-1,))
    north = passed_along(tokens[rows - SLAT :], ("lat",), (1,))
    south = passed_along(tokens[:SLAT], ("lat",), (-1,))
    both = ("lon", "lat")
    nw = passed_along(tokens[rows - SLAT :, cols - SLON :], both, (1, 1))
    ne = passed_along(tokens[rows - SLAT :, :SLON], both, (-1, 1))
    sw = passed_along(tokens[:SLAT, cols - SLON :], both, (1, -1))
    se = passed_along(tokens[:SLAT, :SLON], both, (-1, -1))

    vmem = pl.BlockSpec(memory_space=pltpu.VMEM)
    params = pltpu.CompilerParams(vmem_limit_bytes=VMEM_LIMIT)
    shape = (*key_mask.shape, rows, cols)
    place = jnp.stack([lax.axis_index("lat"), lax.axis_index("lon")]).astype(jnp.int32)
    table = jnp.pad(rel_bias, ((0, 0), (0, 9)))
    bias1, bias2, valid = pl.pallas_call(
        functools.partial(prep_kernel, shape=shape),
        out_shape=[jax.ShapeDtypeStruct((HEADS, 2, WIN, WIN), F32)] * 2 + [jax.ShapeDtypeStruct((21, 1, WIN), F32)],
        in_specs=[pl.BlockSpec(memory_space=pltpu.SMEM), vmem, vmem],
        out_specs=[vmem] * 3,
        scratch_shapes=[pltpu.VMEM((8 * WIN, 384), F32)],
        compiler_params=params,
        cost_estimate=pl.CostEstimate(flops=10**9, bytes_accessed=5 * 10**6, transcendentals=0),
        name="prep",
    )(place, table, key_mask)

    g1, b1 = norm1_gain.reshape(1, C), norm1_bias.reshape(1, C)
    g2, b2 = norm2_gain.reshape(1, C), norm2_bias.reshape(1, C)
    fixed = lambda *s: pl.BlockSpec(s, lambda i: (0,) * len(s), pipeline_mode=pl.Buffered(1))
    part = pl.pallas_call(
        inner_kernel,
        grid=((rows - WLAT) // WLAT,),
        out_shape=jax.ShapeDtypeStruct(tokens.shape, BF),
        in_specs=[
            pl.BlockSpec((pl.Element(WLAT), pl.Element(WLON), pl.Element(LEV), pl.Element(C)),
                         lambda i: (SLAT + WLAT * i, SLON, 0, 0)),
            fixed(1, C), fixed(1, C), fixed(C, 3 * C), fixed(HEADS, 2, WIN, WIN), fixed(21, 1, WIN), fixed(C, C),
            fixed(1, C), fixed(1, C), fixed(C, FF), fixed(FF, C),
        ],
        out_specs=pl.BlockSpec((pl.Element(WLAT), pl.Element(WLON), pl.Element(LEV), pl.Element(C)),
                               lambda i: (SLAT + WLAT * i, SLON, 0, 0)),
        scratch_shapes=[pltpu.VMEM((2 * WIN, C), F32), pltpu.VMEM((2 * WIN, C), F32),
                        pltpu.VMEM((2 * WIN, 2 * C), BF), pltpu.VMEM((2 * WIN, C), BF)],
        compiler_params=params,
        cost_estimate=pl.CostEstimate(flops=12 * 10**9, bytes_accessed=12 * 10**6, transcendentals=0),
        name="inner",
    )(tokens, g1, b1, qkv_weight, bias1, valid, proj_weight, g2, b2, fc1_weight, fc2_weight)

    any_space = pl.BlockSpec(memory_space=pl.ANY)
    most = 6 * WIN
    return pl.pallas_call(
        edge_kernel,
        out_shape=jax.ShapeDtypeStruct(tokens.shape, BF),
        in_specs=[any_space] + [vmem] * 20,
        out_specs=any_space,
        scratch_shapes=[pltpu.VMEM((most, C), F32), pltpu.VMEM((most // 2, C), F32), pltpu.VMEM((most, 2 * C), BF),
                        pltpu.VMEM((most // 2, C), F32), pltpu.VMEM((2, 2, WLAT, SLON, LEV, C), BF),
                        pltpu.VMEM((2, SLAT, cols, LEV, C), BF),
                        pltpu.SemaphoreType.DMA((2, 2)), pltpu.SemaphoreType.DMA((2,))],
        input_output_aliases={0: 0},
        compiler_params=params,
        cost_estimate=pl.CostEstimate(flops=16 * 10**9, bytes_accessed=16 * 10**6, transcendentals=0),
        name="edge",
    )(part, tokens, west, east, north, south, nw, ne, sw, se, g1, b1, qkv_weight, bias1, bias2, valid,
      proj_weight, g2, b2, fc1_weight, fc2_weight)


def solution(mesh):
    return jax.shard_map(
        per_device,
        mesh=mesh,
        in_specs=(P("lat", "lon", None, None),) + (P(),) * 10,
        out_specs=P("lat", "lon", None, None),
        check_vma=False,
    )
```

```python
import functools
import math

import jax
import jax.numpy as jnp
import numpy as np
from jax import lax
from jax.experimental import pallas as pl
from jax.experimental.pallas import tpu as pltpu
from jax.sharding import PartitionSpec as P

C = 512
FF = 2048
HEADS = 8
HEAD_DIM = 64
WLEV = 2
WLAT = 6
WLON = 12
LEV = 4
SLAT = 3
SLON = 6
WIN = WLAT * WLON * WLEV
HALF = WIN // 2
QUART = WIN // 4
EPS = 1e-5
LOG2E = math.log2(math.e)
NEG = -jnp.inf
BF = jnp.bfloat16
F32 = jnp.float32
PAIRS = ((1, 2), (3, 0))
VMEM_LIMIT = 56 * 1024 * 1024


def order_columns():
    first = [(p, 6 * h + q, r) for h in range(2) for r in range(2) for p in range(6) for q in range(6)]
    second = [(3 * h + p, q, r) for h in range(2) for r in range(2) for p in range(3) for q in range(12)]
    return first, second


def lane_pqr(u, which):
    half, r, cell = u // HALF, (u // QUART) % 2, u % QUART
    if which == 0:
        return cell // 6, 6 * half + cell % 6, r
    return 3 * half + cell // 12, cell % 12, r


def prep_kernel(place_ref, table_ref, mask_ref, bias1_ref, bias2_ref, valid_ref, rows_ref, *, shape):
    lat, lon, lats = place_ref[0], place_ref[1], shape[0] // shape[2]
    table = table_ref[...] * LOG2E
    out_refs = (bias1_ref, bias2_ref)
    for which, order in enumerate(order_columns()):
        for t, (p, q, r) in enumerate(order):
            start = p * 69 + q * 3 + r
            rows_ref[8 * t : 8 * t + 8, :] = table[:, start : start + 384]
        rows = rows_ref[...]
        high = rows.astype(BF)
        low = (rows - high.astype(F32)).astype(BF)
        k = lax.broadcasted_iota(jnp.int32, (384, WIN), 0)
        p, q, r = lane_pqr(lax.broadcasted_iota(jnp.int32, (384, WIN), 1), which)
        pick = (k == 379 - (p * 69 + q * 3 + r)).astype(F32).astype(BF)
        full = jnp.dot(high, pick, preferred_element_type=F32) + jnp.dot(low, pick, preferred_element_type=F32)
        full = jnp.transpose(full.reshape(WIN, HEADS, WIN), (1, 0, 2))
        out_refs[which][...] = full
    nlat, nlon, tile_rows, tile_cols = shape
    row = lax.broadcasted_iota(jnp.int32, (48, nlat), 0)
    col = lax.broadcasted_iota(jnp.int32, (48, nlat), 1)
    want = lax.rem(lat * tile_rows - SLAT + row + nlat, nlat)
    pick_rows = (want == col).astype(F32).astype(BF)
    mask = (mask_ref[...] > 0).astype(F32).astype(BF)
    picked = jnp.dot(pick_rows, mask, preferred_element_type=F32).astype(BF)
    for which in range(2):
        row = lax.broadcasted_iota(jnp.int32, (nlon, 3 * WIN), 0)
        lane = lax.broadcasted_iota(jnp.int32, (nlon, 3 * WIN), 1)
        _, q, _ = lane_pqr(lane % WIN, which)
        want = lax.rem(lon * tile_cols - SLON + 12 * (lane // WIN) + q + nlon, nlon)
        pick_cols = (want == row).astype(F32).astype(BF)
        spread = jnp.dot(picked, pick_cols, preferred_element_type=F32)
        row = lax.broadcasted_iota(jnp.int32, (48, 3 * WIN), 0)
        lane = lax.broadcasted_iota(jnp.int32, (48, 3 * WIN), 1)
        p, _, _ = lane_pqr(lane % WIN, which)
        lane1 = lax.broadcasted_iota(jnp.int32, (1, 3 * WIN), 1)
        for window in (range(1, 6) if which == 0 else (0, 6)):
            value = jnp.sum(jnp.where(row == 6 * window + p, spread, 0.0), axis=0, keepdims=True)
            ok = value > 0.5
            if window == 0:
                ok = ok & ((lat > 0) | (lane1 % WIN >= HALF))
            if window == 6:
                ok = ok & ((lat < lats - 1) | (lane1 % WIN < HALF))
            value = jnp.where(ok, 0.0, NEG)
            for k in range(3):
                valid_ref[3 * window + k] = value[:, k * WIN : (k + 1) * WIN]


def layer_norm(values, gain, offset):
    average = jnp.mean(values, axis=-1, keepdims=True)
    centred = values - average
    spread = jnp.mean(centred * centred, axis=-1, keepdims=True)
    return centred * lax.rsqrt(spread + EPS) * gain + offset


def by_level(block):
    cells = block.astype(F32).reshape(QUART, LEV, C)
    return jnp.transpose(cells, (1, 0, 2))


def from_level(rows, shape):
    return jnp.transpose(rows, (1, 0, 2)).reshape(shape).astype(BF)


def attend(q, k, v, bias_of, block_mask):
    n = q.shape[0]
    head_of = lax.broadcasted_iota(jnp.int32, (1, 256), 1) // HEAD_DIM
    parts = []
    for g in range(2):
        lanes = slice(256 * g, 256 * g + 256)
        qg = q[:, lanes]
        stacked = jnp.concatenate([jnp.where(head_of == j, qg, 0.0) for j in range(4)], axis=0).astype(BF)
        scores = lax.dot_general(stacked, k[:, lanes], (((1,), (1,)), ((), ())), preferred_element_type=F32)
        probs, scale = [], []
        for j in range(4):
            s = scores[j * n : (j + 1) * n] + (bias_of(4 * g + j) + block_mask)
            powered = jnp.exp2(s - jnp.max(s, axis=-1, keepdims=True))
            scale.append(1.0 / jnp.sum(powered, axis=-1, keepdims=True))
            probs.append(powered)
        probs = jnp.concatenate(probs, axis=0).astype(BF)
        out = jnp.dot(probs, v[:, lanes], preferred_element_type=F32)
        context = out[:n] * scale[0]
        for j in range(1, 4):
            context = jnp.where(head_of == j, out[j * n : (j + 1) * n] * scale[j], context)
        parts.append(context)
    return jnp.concatenate(parts, axis=1)


def feed(middle, gain, offset, fc1_ref, fc2_ref):
    normed = layer_norm(middle, gain, offset).astype(BF)
    total = None
    for j in range(4):
        v = jnp.dot(normed, fc1_ref[:, 512 * j : 512 * j + 512], preferred_element_type=F32)
        hidden = (v + v * lax.erf(v * (0.5 ** 0.5))).astype(BF)
        part = jnp.dot(hidden, fc2_ref[512 * j : 512 * j + 512, :], preferred_element_type=F32)
        total = part if total is None else total + part
    return middle + 0.5 * total


def block_masks(valid, first, n):
    t = lax.broadcasted_iota(jnp.int32, (n, WIN), 0) + first
    u = lax.broadcasted_iota(jnp.int32, (n, WIN), 1)
    joint = jnp.where(t == u, 0.0, jnp.broadcast_to(valid, (n, WIN)))
    same = (t // QUART) % 2 == (u // QUART) % 2
    return joint, jnp.where(same, joint, NEG)


def put_levels(levels, into_ref, at, step):
    for pair in range(2):
        rows = jnp.concatenate([levels[level] for level in PAIRS[pair]], axis=0)
        into_ref[pl.ds(pl.multiple_of(at + step * pair, 8), HALF), :] = rows


def take_levels(from_ref, at, step):
    levels = [None] * LEV
    for pair in range(2):
        rows = from_ref[pl.ds(pl.multiple_of(at + step * pair, 8), HALF), :]
        for r in range(2):
            levels[PAIRS[pair][r]] = rows[QUART * r : QUART * r + QUART]
    return jnp.stack(levels)


def rest_of_block(rows, ctx_ref, xs_ref, proj_ref, g2_ref, b2_ref, fc1_ref, fc2_ref):
    moved = jnp.dot(ctx_ref[rows, :], proj_ref[...], preferred_element_type=F32).astype(BF)
    middle = xs_ref[rows, :] + moved.astype(F32)
    xs_ref[rows, :] = feed(middle, g2_ref[...], b2_ref[...], fc1_ref, fc2_ref)


def start_copies(pairs, sem):
    copies = [pltpu.make_async_copy(src, dst, sem.at[n]) for n, (src, dst) in enumerate(pairs)]
    for copy in copies:
        copy.start()
    return copies


Q_SCALE = HEAD_DIM ** -0.5 * LOG2E


def inner_kernel(tok_hbm, qkv_hbm, bias_hbm, proj_hbm, fc1_hbm, fc2_hbm, g1_ref, b1_ref, valid_ref, g2_ref, b2_ref,
                 out_hbm, tok_ref, qkv_ref, bias_ref, proj_ref, fc1_ref, fc2_ref, out_ref, xs_ref, norm_ref, q_ref,
                 kv_ref, ctx_ref, sem, out_sem):
    steps = tok_ref.shape[0] // WLAT
    inner = (pl.ds(SLAT, WLAT * steps), pl.ds(SLON, WLON))
    copies = start_copies([(tok_hbm.at[inner], tok_ref), (qkv_hbm, qkv_ref), (bias_hbm, bias_ref),
                           (proj_hbm, proj_ref), (fc1_hbm, fc1_ref), (fc2_hbm, fc2_ref)], sem)
    big = 2 * WIN
    part = big * steps // 2

    copies[0].wait()

    def load(i, carry):
        at = pl.multiple_of(big * i, big)
        x = tok_ref[pl.ds(WLAT * i, WLAT)]
        for h in range(2):
            put_levels(by_level(x[:, 6 * h : 6 * h + 6]), xs_ref, at + HALF * h, WIN)
        norm_ref[pl.ds(at, big), :] = layer_norm(xs_ref[pl.ds(at, big), :], g1_ref[...], b1_ref[...]).astype(BF)
        return carry

    lax.fori_loop(0, steps, load, 0)
    copies[1].wait()

    def project(i, carry):
        rows = pl.ds(pl.multiple_of(part * i, 16), part)
        normed = norm_ref[rows, :]
        q_ref[rows, :] = jnp.dot(normed, qkv_ref[:, :C], preferred_element_type=F32) * Q_SCALE
        kv_ref[rows, :] = jnp.dot(normed, qkv_ref[:, C:], preferred_element_type=F32).astype(BF)
        return carry

    lax.fori_loop(0, 2, project, 0)
    copies[2].wait()

    def attention(i, carry):
        masks = block_masks(valid_ref[3 * (i + 1) + 1], 0, WIN)
        for pair in range(2):
            rows = pl.ds(pl.multiple_of(big * i + WIN * pair, WIN), WIN)
            ctx_ref[rows, :] = attend(q_ref[rows, :], kv_ref[rows, :C], kv_ref[rows, C:],
                                      lambda h: bias_ref[h], masks[pair]).astype(BF)
        return carry

    lax.fori_loop(0, steps, attention, 0)
    for copy in copies[3:]:
        copy.wait()

    def rest(i, carry):
        rest_of_block(pl.ds(pl.multiple_of(part * i, 16), part), ctx_ref, xs_ref, proj_ref, g2_ref, b2_ref,
                      fc1_ref, fc2_ref)
        return carry

    lax.fori_loop(0, 2, rest, 0)

    def store(i, carry):
        for h in range(2):
            levels = take_levels(xs_ref, pl.multiple_of(big * i, big) + HALF * h, WIN)
            out_ref[pl.ds(WLAT * i, WLAT), 6 * h : 6 * h + 6] = from_level(levels, (WLAT, 6, LEV, C))
        return carry

    lax.fori_loop(0, steps, store, 0)
    out = pltpu.make_async_copy(out_ref, out_hbm.at[inner], out_sem)
    out.start()
    out.wait()


def edge_kernel(part_hbm, tok_hbm, west_hbm, east_hbm, north_hbm, south_hbm, qkv_hbm, bias1_hbm, bias2_hbm, proj_hbm,
                fc1_hbm, fc2_hbm, g1_ref, b1_ref, valid_ref, g2_ref, b2_ref, out_hbm,
                own_ref, strip_ref, west_ref, east_ref, north_ref, south_ref, qkv_ref, bias1_ref, bias2_ref, proj_ref,
                fc1_ref, fc2_ref, xs_ref, q_ref, kv_ref, ctx_ref, mid_ref, sem, out_sem):
    del part_hbm
    rows, cols = tok_hbm.shape[:2]
    steps = (rows - WLAT) // WLAT
    side_at = ((pl.ds(SLAT, WLAT * steps), pl.ds(0, SLON)), (pl.ds(SLAT, WLAT * steps), pl.ds(cols - SLON, SLON)))
    strip_at = (pl.ds(0, SLAT), pl.ds(rows - SLAT, SLAT))
    places = [(own_ref.at[side], side_at[side]) for side in range(2)]
    places += [(strip_ref.at[which], strip_at[which]) for which in range(2)]
    copies = start_copies([(tok_hbm.at[at], here) for here, at in places[:2]] + [
        (west_hbm, west_ref), (east_hbm, east_ref), (qkv_hbm, qkv_ref), (bias1_hbm, bias1_ref)] + [
        (tok_hbm.at[at], here) for here, at in places[2:]] + [
        (north_hbm, north_ref), (south_hbm, south_ref), (bias2_hbm, bias2_ref), (proj_hbm, proj_ref),
        (fc1_hbm, fc1_ref), (fc2_hbm, fc2_ref)], sem)
    big = 2 * WIN

    def normed_rows(ref, first, count):
        return layer_norm(ref[first : first + count, :], g1_ref[...], b1_ref[...])

    for copy in copies[:6]:
        copy.wait()

    def sides(i, carry):
        at = pl.multiple_of(big * i, big)
        own_rows, halo_rows = pl.ds(WLAT * i, WLAT), pl.ds(2 * SLAT + WLAT * i, WLAT)
        for side, halo_ref in ((0, west_ref), (1, east_ref)):
            own = by_level(own_ref[side, own_rows])
            put_levels(own, xs_ref, big * side + (HALF if side == 0 else 0), WIN)
            put_levels(by_level(halo_ref[halo_rows]), xs_ref, big * side + (0 if side == 0 else HALF), WIN)
            put_levels(own, mid_ref, at + WIN * side, HALF)
        normed = normed_rows(xs_ref, 0, 2 * big)
        kv_ref[: 2 * big, :] = jnp.dot(normed.astype(BF), qkv_ref[:, C:], preferred_element_type=F32).astype(BF)
        own = jnp.concatenate([normed[HALF:WIN], normed[WIN + HALF : big], normed[big : big + HALF],
                               normed[big + WIN : big + WIN + HALF]], axis=0)
        q_ref[...] = jnp.dot(own.astype(BF), qkv_ref[:, :C], preferred_element_type=F32) * Q_SCALE
        contexts = []
        for side in range(2):
            first = HALF if side == 0 else 0
            masks = block_masks(valid_ref[3 * (i + 1) + 2 * side], first, HALF)
            for pair in range(2):
                mine, keys = WIN * side + HALF * pair, big * side + WIN * pair
                contexts.append(attend(q_ref[mine : mine + HALF, :], kv_ref[keys : keys + WIN, :C],
                                       kv_ref[keys : keys + WIN, C:],
                                       lambda h: bias1_ref[h, first : first + HALF, :], masks[pair]))
        ctx_ref[pl.ds(at, big), :] = jnp.concatenate(contexts, axis=0).astype(BF)
        return carry

    lax.fori_loop(0, steps, sides, 0)
    for copy in copies[6:11]:
        copy.wait()

    for which in range(2):
        at = big * (steps + which)
        first = HALF if which == 0 else 0
        inside = slice(SLAT, 2 * SLAT) if which == 0 else slice(rows, rows + SLAT)
        outside = slice(0, SLAT) if which == 0 else slice(rows + SLAT, rows + 2 * SLAT)
        near_ref = (north_ref, south_ref)[which]
        own = jnp.concatenate([west_ref[inside], strip_ref[which], east_ref[inside]], axis=1)
        halo = jnp.concatenate([west_ref[outside], near_ref[...], east_ref[outside]], axis=1)
        for k in range(3):
            window = slice(WLON * k, WLON * k + WLON)
            put_levels(by_level(own[:, window]), xs_ref, big * k + first, WIN)
            put_levels(by_level(halo[:, window]), xs_ref, big * k + HALF - first, WIN)
            if k == 1:
                put_levels(by_level(own[:, window]), mid_ref, at, HALF)
        corner = jnp.concatenate([strip_ref[which, :, cols - SLON :], strip_ref[which, :, :SLON]], axis=1)
        put_levels(by_level(corner), mid_ref, at + WIN, HALF)
        kv_ref[...] = jnp.dot(normed_rows(xs_ref, 0, 3 * big).astype(BF), qkv_ref[:, C:],
                              preferred_element_type=F32).astype(BF)
        q_ref[...] = jnp.dot(normed_rows(mid_ref, at, big).astype(BF), qkv_ref[:, :C],
                             preferred_element_type=F32) * Q_SCALE
        contexts = {}
        for k in range(3):
            masks = block_masks(valid_ref[18 * which + k], first, HALF)
            for pair in range(2):
                mine, keys = (0 if k == 1 else WIN) + HALF * pair, big * k + WIN * pair
                contexts[k, pair] = attend(q_ref[mine : mine + HALF, :], kv_ref[keys : keys + WIN, :C],
                                           kv_ref[keys : keys + WIN, C:],
                                           lambda h: bias2_ref[h, first : first + HALF, :], masks[pair])
        east_cell = lax.broadcasted_iota(jnp.int32, (HALF, 1), 0) % WLON < SLON
        ctx_ref[at : at + big, :] = jnp.concatenate(
            [contexts[1, 0], contexts[1, 1]] + [jnp.where(east_cell, contexts[2, pair], contexts[0, pair])
                                                for pair in range(2)], axis=0).astype(BF)
    for copy in copies[11:]:
        copy.wait()
    part = big * (steps + 2) // 3

    def rest(i, carry):
        rest_of_block(pl.ds(pl.multiple_of(part * i, 16), part), ctx_ref, mid_ref, proj_ref, g2_ref, b2_ref,
                      fc1_ref, fc2_ref)
        return carry

    lax.fori_loop(0, 3, rest, 0)

    def store(i, carry):
        at = pl.multiple_of(big * i, big)
        for side in range(2):
            block = from_level(take_levels(mid_ref, at + WIN * side, HALF), (WLAT, SLON, LEV, C))
            own_ref[side, pl.ds(WLAT * i, WLAT)] = block
        return carry

    lax.fori_loop(0, steps, store, 0)
    for which in range(2):
        at = big * (steps + which)
        strip_ref[which, :, SLON : SLON + WLON] = from_level(take_levels(mid_ref, at, HALF), (SLAT, WLON, LEV, C))
        block = from_level(take_levels(mid_ref, at + WIN, HALF), (SLAT, WLON, LEV, C))
        strip_ref[which, :, cols - SLON :] = block[:, :SLON]
        strip_ref[which, :, :SLON] = block[:, SLON:]
    outs = start_copies([(here, out_hbm.at[at]) for here, at in places], out_sem)
    for copy in outs:
        copy.wait()


def passed_along(block, axis, distance):
    size = lax.axis_size(axis)
    return lax.ppermute(block, axis, [((i - distance) % size, i) for i in range(size)])


def per_device(tokens, norm1_gain, norm1_bias, qkv_weight, rel_bias, key_mask, proj_weight,
               norm2_gain, norm2_bias, fc1_weight, fc2_weight):
    rows, cols = tokens.shape[:2]
    north = passed_along(tokens[rows - SLAT :], "lat", 1)
    south = passed_along(tokens[:SLAT], "lat", -1)

    vmem = pl.BlockSpec(memory_space=pltpu.VMEM)
    any_space = pl.BlockSpec(memory_space=pl.ANY)
    params = pltpu.CompilerParams(vmem_limit_bytes=VMEM_LIMIT)
    shape = (*key_mask.shape, rows, cols)
    place = jnp.stack([lax.axis_index("lat"), lax.axis_index("lon")]).astype(jnp.int32)
    table = jnp.pad(rel_bias, ((0, 0), (0, 9)))
    bias1, bias2, valid = pl.pallas_call(
        functools.partial(prep_kernel, shape=shape),
        out_shape=[jax.ShapeDtypeStruct((HEADS, WIN, WIN), F32)] * 2 + [jax.ShapeDtypeStruct((21, 1, WIN), F32)],
        in_specs=[pl.BlockSpec(memory_space=pltpu.SMEM), vmem, vmem],
        out_specs=[vmem] * 3,
        scratch_shapes=[pltpu.VMEM((8 * WIN, 384), F32)],
        compiler_params=params,
        cost_estimate=pl.CostEstimate(flops=10**9, bytes_accessed=5 * 10**6, transcendentals=0),
        name="prep",
    )(place, table, key_mask)

    def column(at):
        return jnp.concatenate([north[:, at], tokens[:, at], south[:, at]], axis=0)

    west = passed_along(column(slice(cols - SLON, cols)), "lon", 1)
    east = passed_along(column(slice(0, SLON)), "lon", -1)

    g1, b1 = norm1_gain.reshape(1, C), norm1_bias.reshape(1, C)
    g2, b2 = norm2_gain.reshape(1, C), norm2_bias.reshape(1, C)
    count = 2 * WIN * ((rows - WLAT) // WLAT)
    weights = [pltpu.VMEM((C, C), BF), pltpu.VMEM((C, FF), BF), pltpu.VMEM((FF, C), BF)]
    table_shape = pltpu.VMEM((HEADS, WIN, WIN), F32)
    inner_shape = pltpu.VMEM((rows - 2 * SLAT, WLON, LEV, C), BF)
    part = pl.pallas_call(
        inner_kernel,
        out_shape=jax.ShapeDtypeStruct(tokens.shape, BF),
        in_specs=[any_space] * 6 + [vmem] * 5,
        out_specs=any_space,
        scratch_shapes=[inner_shape, pltpu.VMEM((C, 3 * C), BF), table_shape, *weights, inner_shape,
                        pltpu.VMEM((count, C), F32), pltpu.VMEM((count, C), BF), pltpu.VMEM((count, C), F32),
                        pltpu.VMEM((count, 2 * C), BF), pltpu.VMEM((count, C), BF),
                        pltpu.SemaphoreType.DMA((6,)), pltpu.SemaphoreType.DMA],
        compiler_params=params,
        cost_estimate=pl.CostEstimate(flops=12 * 10**9, bytes_accessed=12 * 10**6, transcendentals=0),
        name="inner",
    )(tokens, qkv_weight, bias1, proj_weight, fc1_weight, fc2_weight, g1, b1, valid, g2, b2)

    own = count + 4 * WIN
    strip = (SLAT, cols, LEV, C)
    halo = (rows + 2 * SLAT, SLON, LEV, C)
    return pl.pallas_call(
        edge_kernel,
        out_shape=jax.ShapeDtypeStruct(tokens.shape, BF),
        in_specs=[any_space] * 12 + [vmem] * 5,
        out_specs=any_space,
        scratch_shapes=[pltpu.VMEM((2, rows - 2 * SLAT, SLON, LEV, C), BF), pltpu.VMEM((2, *strip), BF),
                        pltpu.VMEM(halo, BF), pltpu.VMEM(halo, BF), pltpu.VMEM(strip, BF), pltpu.VMEM(strip, BF),
                        pltpu.VMEM((C, 3 * C), BF), table_shape, table_shape, *weights,
                        pltpu.VMEM((6 * WIN, C), F32), pltpu.VMEM((2 * WIN, C), F32), pltpu.VMEM((6 * WIN, 2 * C), BF),
                        pltpu.VMEM((own, C), BF), pltpu.VMEM((own, C), F32),
                        pltpu.SemaphoreType.DMA((14,)), pltpu.SemaphoreType.DMA((4,))],
        input_output_aliases={0: 0},
        compiler_params=params,
        cost_estimate=pl.CostEstimate(flops=16 * 10**9, bytes_accessed=16 * 10**6, transcendentals=0),
        name="edge",
    )(part, tokens, west, east, north, south, qkv_weight, bias1, bias2, proj_weight, fc1_weight, fc2_weight,
      g1, b1, valid, g2, b2)


def solution(mesh):
    return jax.shard_map(
        per_device,
        mesh=mesh,
        in_specs=(P("lat", "lon", None, None),) + (P(),) * 10,
        out_specs=P("lat", "lon", None, None),
        check_vma=False,
    )
```

```python
import functools
import math

import jax
import jax.numpy as jnp
import numpy as np
from jax import lax
from jax.experimental import pallas as pl
from jax.experimental.pallas import tpu as pltpu
from jax.sharding import PartitionSpec as P

C = 512
FF = 2048
HEADS = 8
HEAD_DIM = 64
WLEV = 2
WLAT = 6
WLON = 12
LEV = 4
SLAT = 3
SLON = 6
WIN = WLAT * WLON * WLEV
HALF = WIN // 2
QUART = WIN // 4
EPS = 1e-5
LOG2E = math.log2(math.e)
NEG = -jnp.inf
BF = jnp.bfloat16
F32 = jnp.float32
PAIRS = ((1, 2), (3, 0))
VMEM_LIMIT = 44 * 1024 * 1024


def order_columns():
    first = [(p, 6 * h + q, r) for h in range(2) for r in range(2) for p in range(6) for q in range(6)]
    second = [(3 * h + p, q, r) for h in range(2) for r in range(2) for p in range(3) for q in range(12)]
    return first, second


def lane_pqr(u, which):
    half, r, cell = u // HALF, (u // QUART) % 2, u % QUART
    if which == 0:
        return cell // 6, 6 * half + cell % 6, r
    return 3 * half + cell // 12, cell % 12, r


def prep_kernel(table_ref, mask_ref, tok_hbm, bias1_ref, bias2_ref, valid_ref, low_hbm, high_hbm,
                wide_ref, rows_ref, sem, *, shape):
    nlat, nlon, tile_rows, tile_cols = shape
    copies = start_copies([(tok_hbm.at[:, pl.ds(0, SLON)], low_hbm),
                           (tok_hbm.at[:, pl.ds(tile_cols - SLON, SLON)], high_hbm)], sem)
    lat, lon, lats = lax.axis_index("lat"), lax.axis_index("lon"), nlat // tile_rows
    first, second = order_columns()
    wide_ref[...] = jnp.zeros_like(wide_ref)
    wide_ref[:, : table_ref.shape[1]] = table_ref[...] * LOG2E
    for t, (p, q, r) in enumerate(first):
        start = p * 69 + q * 3 + r
        rows_ref[8 * t : 8 * t + 8, :] = wide_ref[:, start : start + 384]
    rows = rows_ref[...]
    high = rows.astype(BF)
    low = (rows - high.astype(F32)).astype(BF)
    k = lax.broadcasted_iota(jnp.int32, (384, WIN), 0)
    for which, out_ref in enumerate((bias1_ref, bias2_ref)):
        p, q, r = lane_pqr(lax.broadcasted_iota(jnp.int32, (1, WIN), 1), which)
        pick = jnp.where(k == 379 - (p * 69 + q * 3 + r), 1.0, 0.0).astype(BF)
        full = jnp.dot(high, pick, preferred_element_type=F32) + jnp.dot(low, pick, preferred_element_type=F32)
        full = full.reshape(WIN, HEADS, WIN)
        if which == 1:
            full = jnp.stack([full[first.index(pqr)] for pqr in second])
        out_ref[...] = jnp.transpose(full, (1, 0, 2))
    row = lax.broadcasted_iota(jnp.int32, (48, 1), 0)
    col = lax.broadcasted_iota(jnp.int32, (48, nlat), 1)
    want = lax.rem(lat * tile_rows - SLAT + row + nlat, nlat)
    pick_rows = jnp.where(want == col, 1.0, 0.0).astype(BF)
    mask = (mask_ref[...] > 0).astype(F32).astype(BF)
    picked = jnp.dot(pick_rows, mask, preferred_element_type=F32).astype(BF)
    row = lax.broadcasted_iota(jnp.int32, (nlon, 3 * WIN), 0)
    row48 = lax.broadcasted_iota(jnp.int32, (48, 3 * WIN), 0)
    lane = lax.broadcasted_iota(jnp.int32, (1, 3 * WIN), 1)
    for which in range(2):
        p, q, _ = lane_pqr(lane % WIN, which)
        want = lax.rem(lon * tile_cols - SLON + 12 * (lane // WIN) + q + nlon, nlon)
        pick_cols = jnp.where(want == row, 1.0, 0.0).astype(BF)
        spread = jnp.dot(picked, pick_cols, preferred_element_type=F32)
        for window in (range(1, 6) if which == 0 else (0, 6)):
            value = jnp.sum(jnp.where(row48 == 6 * window + p, spread, 0.0), axis=0, keepdims=True)
            ok = value > 0.5
            if window == 0:
                ok = ok & ((lat > 0) | (lane % WIN >= HALF))
            if window == 6:
                ok = ok & ((lat < lats - 1) | (lane % WIN < HALF))
            value = jnp.where(ok, 0.0, NEG)
            for n in range(3):
                valid_ref[3 * window + n] = value[:, n * WIN : (n + 1) * WIN]
    for copy in copies:
        copy.wait()


def layer_norm(values, gain, offset):
    average = jnp.mean(values, axis=-1, keepdims=True)
    centred = values - average
    spread = jnp.mean(centred * centred, axis=-1, keepdims=True)
    return centred * lax.rsqrt(spread + EPS) * gain + offset


def by_level(block):
    cells = block.astype(F32).reshape(QUART, LEV, C)
    return jnp.transpose(cells, (1, 0, 2))


def from_level(rows, shape):
    return jnp.transpose(rows, (1, 0, 2)).reshape(shape).astype(BF)


def attend(q, k, v, bias_of, block_mask):
    n = q.shape[0]
    head_of = lax.broadcasted_iota(jnp.int32, (1, 2 * HEAD_DIM), 1) // HEAD_DIM
    ones = jnp.ones((WIN, 2 * HEAD_DIM), BF)
    parts = []
    for g in range(HEADS // 2):
        lanes = slice(2 * HEAD_DIM * g, 2 * HEAD_DIM * (g + 1))
        qg = q[:, lanes]
        stacked = jnp.concatenate([jnp.where(head_of == j, qg, 0.0) for j in range(2)], axis=0).astype(BF)
        scores = lax.dot_general(stacked, k[:, lanes], (((1,), (1,)), ((), ())), preferred_element_type=F32)
        probs = []
        for j in range(2):
            s = scores[j * n : (j + 1) * n] + (bias_of(2 * g + j) + block_mask)
            probs.append(jnp.exp2(s - jnp.max(s, axis=-1, keepdims=True)))
        probs = jnp.concatenate(probs, axis=0).astype(BF)
        out = jnp.dot(probs, jnp.concatenate([v[:, lanes], ones], axis=1), preferred_element_type=F32)
        out = jnp.where(jnp.concatenate([head_of, head_of], axis=1) == 0, out[:n], out[n:])
        parts.append(out[:, : 2 * HEAD_DIM] / out[:, 2 * HEAD_DIM :])
    return jnp.concatenate(parts, axis=1)


def feed(middle, gain, offset, fc1_ref, fc2_ref):
    normed = layer_norm(middle, gain, offset).astype(BF)
    total = None
    for j in range(4):
        v = jnp.dot(normed, fc1_ref[:, 512 * j : 512 * j + 512], preferred_element_type=F32)
        hidden = (v + v * lax.erf(v * (0.5 ** 0.5))).astype(BF)
        part = jnp.dot(hidden, fc2_ref[512 * j : 512 * j + 512, :], preferred_element_type=F32)
        total = part if total is None else total + part
    return middle + 0.5 * total


def block_masks(valid, first, n):
    t = lax.broadcasted_iota(jnp.int32, (n, 1), 0) + first
    u = lax.broadcasted_iota(jnp.int32, (1, WIN), 1)
    joint = jnp.where(t == u, 0.0, jnp.broadcast_to(valid, (n, WIN)))
    same = (t // QUART) % 2 == (u // QUART) % 2
    return joint, jnp.where(same, joint, NEG)


def put_levels(levels, into_ref, at, step):
    for pair in range(2):
        rows = jnp.concatenate([levels[level] for level in PAIRS[pair]], axis=0)
        into_ref[pl.ds(pl.multiple_of(at + step * pair, 8), HALF), :] = rows


def take_levels(from_ref, at, step):
    levels = [None] * LEV
    for pair in range(2):
        rows = from_ref[pl.ds(pl.multiple_of(at + step * pair, 8), HALF), :]
        for r in range(2):
            levels[PAIRS[pair][r]] = rows[QUART * r : QUART * r + QUART]
    return jnp.stack(levels)


def rest_of_block(rows, ctx_ref, xs_ref, proj_ref, g2_ref, b2_ref, fc1_ref, fc2_ref):
    moved = jnp.dot(ctx_ref[rows, :], proj_ref[...], preferred_element_type=F32).astype(BF)
    middle = xs_ref[rows, :] + moved.astype(F32)
    xs_ref[rows, :] = feed(middle, g2_ref[...], b2_ref[...], fc1_ref, fc2_ref)


def start_copies(pairs, sem):
    copies = [pltpu.make_async_copy(src, dst, sem.at[n]) for n, (src, dst) in enumerate(pairs)]
    for copy in copies:
        copy.start()
    return copies


Q_SCALE = HEAD_DIM ** -0.5 * LOG2E


def inner_kernel(tok_hbm, qkv_hbm, bias_hbm, proj_hbm, fc1_hbm, fc2_hbm, g1_ref, b1_ref, valid_ref, g2_ref, b2_ref,
                 out_hbm, tok_ref, qkv_ref, bias_ref, proj_ref, fc1_ref, fc2_ref, out_ref, xs_ref, norm_ref, q_ref,
                 kv_ref, ctx_ref, sem, out_sem):
    steps = tok_ref.shape[0] // WLAT
    inner = (pl.ds(SLAT, WLAT * steps), pl.ds(SLON, WLON))
    copies = start_copies([(tok_hbm.at[inner], tok_ref), (qkv_hbm, qkv_ref), (bias_hbm, bias_ref),
                           (proj_hbm, proj_ref), (fc1_hbm, fc1_ref), (fc2_hbm, fc2_ref)], sem)
    big = 2 * WIN
    part = big * steps // 2

    copies[0].wait()

    def load(i, carry):
        at = pl.multiple_of(big * i, big)
        x = tok_ref[pl.ds(WLAT * i, WLAT)]
        for h in range(2):
            put_levels(by_level(x[:, 6 * h : 6 * h + 6]), xs_ref, at + HALF * h, WIN)
        norm_ref[pl.ds(at, big), :] = layer_norm(xs_ref[pl.ds(at, big), :], g1_ref[...], b1_ref[...]).astype(BF)
        return carry

    lax.fori_loop(0, steps, load, 0)
    copies[1].wait()

    def project(i, carry):
        rows = pl.ds(pl.multiple_of(part * i, 16), part)
        normed = norm_ref[rows, :]
        q_ref[rows, :] = jnp.dot(normed, qkv_ref[:, :C], preferred_element_type=F32) * Q_SCALE
        kv_ref[rows, :] = jnp.dot(normed, qkv_ref[:, C:], preferred_element_type=F32).astype(BF)
        return carry

    lax.fori_loop(0, 2, project, 0)
    copies[2].wait()

    def attention(i, carry):
        masks = block_masks(valid_ref[3 * (i + 1) + 1], 0, WIN)
        for pair in range(2):
            rows = pl.ds(pl.multiple_of(big * i + WIN * pair, WIN), WIN)
            ctx_ref[rows, :] = attend(q_ref[rows, :], kv_ref[rows, :C], kv_ref[rows, C:],
                                      lambda h: bias_ref[h], masks[pair]).astype(BF)
        return carry

    lax.fori_loop(0, steps, attention, 0)
    for copy in copies[3:]:
        copy.wait()

    def rest(i, carry):
        rest_of_block(pl.ds(pl.multiple_of(part * i, 16), part), ctx_ref, xs_ref, proj_ref, g2_ref, b2_ref,
                      fc1_ref, fc2_ref)
        return carry

    lax.fori_loop(0, 2, rest, 0)

    def store(i, carry):
        for h in range(2):
            levels = take_levels(xs_ref, pl.multiple_of(big * i, big) + HALF * h, WIN)
            out_ref[pl.ds(WLAT * i, WLAT), 6 * h : 6 * h + 6] = from_level(levels, (WLAT, 6, LEV, C))
        return carry

    lax.fori_loop(0, steps, store, 0)
    out = pltpu.make_async_copy(out_ref, out_hbm.at[inner], out_sem)
    out.start()
    out.wait()


def edge_kernel(part_hbm, tok_hbm, west_hbm, east_hbm, north_hbm, south_hbm, qkv_hbm, bias1_hbm, bias2_hbm, proj_hbm,
                fc1_hbm, fc2_hbm, g1_ref, b1_ref, valid_ref, g2_ref, b2_ref, out_hbm,
                own_ref, strip_ref, west_ref, east_ref, north_ref, south_ref, qkv_ref, bias1_ref, bias2_ref, proj_ref,
                fc1_ref, fc2_ref, xs_ref, q_ref, kv_ref, ctx_ref, mid_ref, sem, out_sem):
    del part_hbm
    rows, cols = tok_hbm.shape[:2]
    steps = (rows - WLAT) // WLAT
    side_at = ((pl.ds(SLAT, WLAT * steps), pl.ds(0, SLON)), (pl.ds(SLAT, WLAT * steps), pl.ds(cols - SLON, SLON)))
    strip_at = (pl.ds(0, SLAT), pl.ds(rows - SLAT, SLAT))
    places = [(own_ref.at[side], side_at[side]) for side in range(2)]
    places += [(strip_ref.at[which], strip_at[which]) for which in range(2)]
    copies = start_copies([(tok_hbm.at[at], here) for here, at in places[:2]] + [
        (west_hbm, west_ref), (east_hbm, east_ref), (qkv_hbm, qkv_ref), (bias1_hbm, bias1_ref)] + [
        (tok_hbm.at[at], here) for here, at in places[2:]] + [
        (north_hbm, north_ref), (south_hbm, south_ref), (bias2_hbm, bias2_ref), (proj_hbm, proj_ref),
        (fc1_hbm, fc1_ref), (fc2_hbm, fc2_ref)], sem)
    big = 2 * WIN

    def normed_rows(ref, first, count):
        return layer_norm(ref[first : first + count, :], g1_ref[...], b1_ref[...])

    for copy in copies[:6]:
        copy.wait()

    def sides(i, carry):
        at = pl.multiple_of(big * i, big)
        own_rows, halo_rows = pl.ds(WLAT * i, WLAT), pl.ds(2 * SLAT + WLAT * i, WLAT)
        for side, halo_ref in ((0, west_ref), (1, east_ref)):
            own = by_level(own_ref[side, own_rows])
            put_levels(own, xs_ref, big * side + (HALF if side == 0 else 0), WIN)
            put_levels(by_level(halo_ref[halo_rows]), xs_ref, big * side + (0 if side == 0 else HALF), WIN)
            put_levels(own, mid_ref, at + WIN * side, HALF)
        normed = normed_rows(xs_ref, 0, 2 * big)
        kv_ref[: 2 * big, :] = jnp.dot(normed.astype(BF), qkv_ref[:, C:], preferred_element_type=F32).astype(BF)
        own = jnp.concatenate([normed[HALF:WIN], normed[WIN + HALF : big], normed[big : big + HALF],
                               normed[big + WIN : big + WIN + HALF]], axis=0)
        q_ref[...] = jnp.dot(own.astype(BF), qkv_ref[:, :C], preferred_element_type=F32) * Q_SCALE
        contexts = []
        for side in range(2):
            first = HALF if side == 0 else 0
            masks = block_masks(valid_ref[3 * (i + 1) + 2 * side], first, HALF)
            for pair in range(2):
                mine, keys = WIN * side + HALF * pair, big * side + WIN * pair
                contexts.append(attend(q_ref[mine : mine + HALF, :], kv_ref[keys : keys + WIN, :C],
                                       kv_ref[keys : keys + WIN, C:],
                                       lambda h: bias1_ref[h, first : first + HALF, :], masks[pair]))
        ctx_ref[pl.ds(at, big), :] = jnp.concatenate(contexts, axis=0).astype(BF)
        return carry

    lax.fori_loop(0, steps, sides, 0)
    for copy in copies[6:11]:
        copy.wait()

    for which in range(2):
        at = big * (steps + which)
        first = HALF if which == 0 else 0
        inside = slice(SLAT, 2 * SLAT) if which == 0 else slice(rows, rows + SLAT)
        outside = slice(0, SLAT) if which == 0 else slice(rows + SLAT, rows + 2 * SLAT)
        near_ref = (north_ref, south_ref)[which]
        own = jnp.concatenate([west_ref[inside], strip_ref[which], east_ref[inside]], axis=1)
        halo = jnp.concatenate([west_ref[outside], near_ref[...], east_ref[outside]], axis=1)
        for k in range(3):
            window = slice(WLON * k, WLON * k + WLON)
            put_levels(by_level(own[:, window]), xs_ref, big * k + first, WIN)
            put_levels(by_level(halo[:, window]), xs_ref, big * k + HALF - first, WIN)
            if k == 1:
                put_levels(by_level(own[:, window]), mid_ref, at, HALF)
        corner = jnp.concatenate([strip_ref[which, :, cols - SLON :], strip_ref[which, :, :SLON]], axis=1)
        put_levels(by_level(corner), mid_ref, at + WIN, HALF)
        kv_ref[...] = jnp.dot(normed_rows(xs_ref, 0, 3 * big).astype(BF), qkv_ref[:, C:],
                              preferred_element_type=F32).astype(BF)
        q_ref[...] = jnp.dot(normed_rows(mid_ref, at, big).astype(BF), qkv_ref[:, :C],
                             preferred_element_type=F32) * Q_SCALE
        contexts = {}
        for k in range(3):
            masks = block_masks(valid_ref[18 * which + k], first, HALF)
            for pair in range(2):
                mine, keys = (0 if k == 1 else WIN) + HALF * pair, big * k + WIN * pair
                contexts[k, pair] = attend(q_ref[mine : mine + HALF, :], kv_ref[keys : keys + WIN, :C],
                                           kv_ref[keys : keys + WIN, C:],
                                           lambda h: bias2_ref[h, first : first + HALF, :], masks[pair])
        east_cell = lax.broadcasted_iota(jnp.int32, (HALF, 1), 0) % WLON < SLON
        ctx_ref[at : at + big, :] = jnp.concatenate(
            [contexts[1, 0], contexts[1, 1]] + [jnp.where(east_cell, contexts[2, pair], contexts[0, pair])
                                                for pair in range(2)], axis=0).astype(BF)
    for copy in copies[11:]:
        copy.wait()
    part = big * (steps + 2) // 3

    def rest(i, carry):
        rest_of_block(pl.ds(pl.multiple_of(part * i, 16), part), ctx_ref, mid_ref, proj_ref, g2_ref, b2_ref,
                      fc1_ref, fc2_ref)
        return carry

    lax.fori_loop(0, 3, rest, 0)

    def store(i, carry):
        at = pl.multiple_of(big * i, big)
        for side in range(2):
            block = from_level(take_levels(mid_ref, at + WIN * side, HALF), (WLAT, SLON, LEV, C))
            own_ref[side, pl.ds(WLAT * i, WLAT)] = block
        return carry

    lax.fori_loop(0, steps, store, 0)
    for which in range(2):
        at = big * (steps + which)
        strip_ref[which, :, SLON : SLON + WLON] = from_level(take_levels(mid_ref, at, HALF), (SLAT, WLON, LEV, C))
        block = from_level(take_levels(mid_ref, at + WIN, HALF), (SLAT, WLON, LEV, C))
        strip_ref[which, :, cols - SLON :] = block[:, :SLON]
        strip_ref[which, :, :SLON] = block[:, SLON:]
    outs = start_copies([(here, out_hbm.at[at]) for here, at in places], out_sem)
    for copy in outs:
        copy.wait()


def passed_along(block, axis, distance):
    size = lax.axis_size(axis)
    return lax.ppermute(block, axis, [((i - distance) % size, i) for i in range(size)])


def per_device(tokens, norm1_gain, norm1_bias, qkv_weight, rel_bias, key_mask, proj_weight,
               norm2_gain, norm2_bias, fc1_weight, fc2_weight):
    rows, cols = tokens.shape[:2]
    north = passed_along(tokens[rows - SLAT :], "lat", 1)
    south = passed_along(tokens[:SLAT], "lat", -1)

    vmem = pl.BlockSpec(memory_space=pltpu.VMEM)
    any_space = pl.BlockSpec(memory_space=pl.ANY)
    params = pltpu.CompilerParams(vmem_limit_bytes=VMEM_LIMIT)
    shape = (*key_mask.shape, rows, cols)
    edge = jax.ShapeDtypeStruct((rows, SLON, LEV, C), BF)
    bias1, bias2, valid, low, high = pl.pallas_call(
        functools.partial(prep_kernel, shape=shape),
        out_shape=[jax.ShapeDtypeStruct((HEADS, WIN, WIN), F32)] * 2 + [jax.ShapeDtypeStruct((21, 1, WIN), F32)]
        + [edge] * 2,
        in_specs=[vmem, vmem, any_space],
        out_specs=[vmem] * 3 + [any_space] * 2,
        scratch_shapes=[pltpu.VMEM((HEADS, 768), F32), pltpu.VMEM((8 * WIN, 384), F32), pltpu.SemaphoreType.DMA((2,))],
        compiler_params=pltpu.CompilerParams(vmem_limit_bytes=60 * 1024 * 1024),
        cost_estimate=pl.CostEstimate(flops=10**9, bytes_accessed=5 * 10**6, transcendentals=0),
        name="prep",
    )(rel_bias, key_mask, tokens)

    def column(mid, at):
        return jnp.concatenate([north[:, at], mid, south[:, at]], axis=0)

    west = passed_along(column(high, slice(cols - SLON, cols)), "lon", 1)
    east = passed_along(column(low, slice(0, SLON)), "lon", -1)

    g1, b1 = norm1_gain.reshape(1, C), norm1_bias.reshape(1, C)
    g2, b2 = norm2_gain.reshape(1, C), norm2_bias.reshape(1, C)
    count = 2 * WIN * ((rows - WLAT) // WLAT)
    weights = [pltpu.VMEM((C, C), BF), pltpu.VMEM((C, FF), BF), pltpu.VMEM((FF, C), BF)]
    table_shape = pltpu.VMEM((HEADS, WIN, WIN), F32)
    inner_shape = pltpu.VMEM((rows - 2 * SLAT, WLON, LEV, C), BF)
    part = pl.pallas_call(
        inner_kernel,
        out_shape=jax.ShapeDtypeStruct(tokens.shape, BF),
        in_specs=[any_space] * 6 + [vmem] * 5,
        out_specs=any_space,
        scratch_shapes=[inner_shape, pltpu.VMEM((C, 3 * C), BF), table_shape, *weights, inner_shape,
                        pltpu.VMEM((count, C), F32), pltpu.VMEM((count, C), BF), pltpu.VMEM((count, C), F32),
                        pltpu.VMEM((count, 2 * C), BF), pltpu.VMEM((count, C), BF),
                        pltpu.SemaphoreType.DMA((6,)), pltpu.SemaphoreType.DMA],
        compiler_params=params,
        cost_estimate=pl.CostEstimate(flops=12 * 10**9, bytes_accessed=12 * 10**6, transcendentals=0),
        name="inner",
    )(tokens, qkv_weight, bias1, proj_weight, fc1_weight, fc2_weight, g1, b1, valid, g2, b2)

    own = count + 4 * WIN
    strip = (SLAT, cols, LEV, C)
    halo = (rows + 2 * SLAT, SLON, LEV, C)
    return pl.pallas_call(
        edge_kernel,
        out_shape=jax.ShapeDtypeStruct(tokens.shape, BF),
        in_specs=[any_space] * 12 + [vmem] * 5,
        out_specs=any_space,
        scratch_shapes=[pltpu.VMEM((2, rows - 2 * SLAT, SLON, LEV, C), BF), pltpu.VMEM((2, *strip), BF),
                        pltpu.VMEM(halo, BF), pltpu.VMEM(halo, BF), pltpu.VMEM(strip, BF), pltpu.VMEM(strip, BF),
                        pltpu.VMEM((C, 3 * C), BF), table_shape, table_shape, *weights,
                        pltpu.VMEM((6 * WIN, C), F32), pltpu.VMEM((2 * WIN, C), F32), pltpu.VMEM((6 * WIN, 2 * C), BF),
                        pltpu.VMEM((own, C), BF), pltpu.VMEM((own, C), F32),
                        pltpu.SemaphoreType.DMA((14,)), pltpu.SemaphoreType.DMA((4,))],
        input_output_aliases={0: 0},
        compiler_params=params,
        cost_estimate=pl.CostEstimate(flops=16 * 10**9, bytes_accessed=16 * 10**6, transcendentals=0),
        name="edge",
    )(part, tokens, west, east, north, south, qkv_weight, bias1, bias2, proj_weight, fc1_weight, fc2_weight,
      g1, b1, valid, g2, b2)


def solution(mesh):
    return jax.shard_map(
        per_device,
        mesh=mesh,
        in_specs=(P("lat", "lon", None, None),) + (P(),) * 10,
        out_specs=P("lat", "lon", None, None),
        check_vma=False,
    )
```

```python
import functools
import math

import jax
import jax.numpy as jnp
import numpy as np
from jax import lax
from jax.experimental import pallas as pl
from jax.experimental.pallas import tpu as pltpu
from jax.sharding import PartitionSpec as P

C = 512
FF = 2048
HEADS = 8
HEAD_DIM = 64
WLEV = 2
WLAT = 6
WLON = 12
LEV = 4
SLAT = 3
SLON = 6
WIN = WLAT * WLON * WLEV
HALF = WIN // 2
QUART = WIN // 4
EPS = 1e-5
LOG2E = math.log2(math.e)
NEG = -jnp.inf
BF = jnp.bfloat16
F32 = jnp.float32
PAIRS = ((1, 2), (3, 0))
VMEM_LIMIT = 44 * 1024 * 1024


def order_columns():
    first = [(p, 6 * h + q, r) for h in range(2) for r in range(2) for p in range(6) for q in range(6)]
    second = [(3 * h + p, q, r) for h in range(2) for r in range(2) for p in range(3) for q in range(12)]
    return first, second


def lane_pqr(u, which):
    half, r, cell = u // HALF, (u // QUART) % 2, u % QUART
    if which == 0:
        return cell // 6, 6 * half + cell % 6, r
    return 3 * half + cell // 12, cell % 12, r


def prep_kernel(table_ref, mask_ref, bias1_ref, bias2_ref, valid_ref, wide_ref, rows_ref, *, shape):
    nlat, nlon, tile_rows, tile_cols = shape
    lat, lon, lats = lax.axis_index("lat"), lax.axis_index("lon"), nlat // tile_rows
    first, second = order_columns()
    wide_ref[...] = jnp.zeros_like(wide_ref)
    wide_ref[:, : table_ref.shape[1]] = table_ref[...] * LOG2E
    for t, (p, q, r) in enumerate(first):
        start = p * 69 + q * 3 + r
        rows_ref[8 * t : 8 * t + 8, :] = wide_ref[:, start : start + 384]
    rows = rows_ref[...]
    high = rows.astype(BF)
    low = (rows - high.astype(F32)).astype(BF)
    k = lax.broadcasted_iota(jnp.int32, (384, WIN), 0)
    for which, out_ref in enumerate((bias1_ref, bias2_ref)):
        p, q, r = lane_pqr(lax.broadcasted_iota(jnp.int32, (1, WIN), 1), which)
        pick = jnp.where(k == 379 - (p * 69 + q * 3 + r), 1.0, 0.0).astype(BF)
        full = jnp.dot(high, pick, preferred_element_type=F32) + jnp.dot(low, pick, preferred_element_type=F32)
        full = full.reshape(WIN, HEADS, WIN)
        if which == 1:
            full = jnp.stack([full[first.index(pqr)] for pqr in second])
        out_ref[...] = jnp.transpose(full, (1, 0, 2))
    row = lax.broadcasted_iota(jnp.int32, (48, 1), 0)
    col = lax.broadcasted_iota(jnp.int32, (48, nlat), 1)
    want = lax.rem(lat * tile_rows - SLAT + row + nlat, nlat)
    pick_rows = jnp.where(want == col, 1.0, 0.0).astype(BF)
    mask = (mask_ref[...] > 0).astype(F32).astype(BF)
    picked = jnp.dot(pick_rows, mask, preferred_element_type=F32).astype(BF)
    row = lax.broadcasted_iota(jnp.int32, (nlon, 3 * WIN), 0)
    row48 = lax.broadcasted_iota(jnp.int32, (48, 3 * WIN), 0)
    lane = lax.broadcasted_iota(jnp.int32, (1, 3 * WIN), 1)
    for which in range(2):
        p, q, _ = lane_pqr(lane % WIN, which)
        want = lax.rem(lon * tile_cols - SLON + 12 * (lane // WIN) + q + nlon, nlon)
        pick_cols = jnp.where(want == row, 1.0, 0.0).astype(BF)
        spread = jnp.dot(picked, pick_cols, preferred_element_type=F32)
        for window in (range(1, 6) if which == 0 else (0, 6)):
            value = jnp.sum(jnp.where(row48 == 6 * window + p, spread, 0.0), axis=0, keepdims=True)
            ok = value > 0.5
            if window == 0:
                ok = ok & ((lat > 0) | (lane % WIN >= HALF))
            if window == 6:
                ok = ok & ((lat < lats - 1) | (lane % WIN < HALF))
            value = jnp.where(ok, 0.0, NEG)
            for n in range(3):
                valid_ref[3 * window + n] = value[:, n * WIN : (n + 1) * WIN]


def layer_norm(values, gain, offset):
    average = jnp.mean(values, axis=-1, keepdims=True)
    centred = values - average
    spread = jnp.mean(centred * centred, axis=-1, keepdims=True)
    return centred * lax.rsqrt(spread + EPS) * gain + offset


def by_level(block):
    cells = block.astype(F32).reshape(QUART, LEV, C)
    return jnp.transpose(cells, (1, 0, 2))


def from_level(rows, shape):
    return jnp.transpose(rows, (1, 0, 2)).reshape(shape).astype(BF)


def attend(q, k, v, bias_of, block_mask):
    n = q.shape[0]
    head_of = lax.broadcasted_iota(jnp.int32, (1, 2 * HEAD_DIM), 1) // HEAD_DIM
    ones = jnp.ones((WIN, 2 * HEAD_DIM), BF)
    parts = []
    for g in range(HEADS // 2):
        lanes = slice(2 * HEAD_DIM * g, 2 * HEAD_DIM * (g + 1))
        qg = q[:, lanes]
        stacked = jnp.concatenate([jnp.where(head_of == j, qg, 0.0) for j in range(2)], axis=0).astype(BF)
        scores = lax.dot_general(stacked, k[:, lanes], (((1,), (1,)), ((), ())), preferred_element_type=F32)
        probs = []
        for j in range(2):
            s = scores[j * n : (j + 1) * n] + (bias_of(2 * g + j) + block_mask)
            probs.append(jnp.exp2(s - jnp.max(s, axis=-1, keepdims=True)))
        probs = jnp.concatenate(probs, axis=0).astype(BF)
        out = jnp.dot(probs, jnp.concatenate([v[:, lanes], ones], axis=1), preferred_element_type=F32)
        out = jnp.where(jnp.concatenate([head_of, head_of], axis=1) == 0, out[:n], out[n:])
        parts.append(out[:, : 2 * HEAD_DIM] / out[:, 2 * HEAD_DIM :])
    return jnp.concatenate(parts, axis=1)


def feed(middle, gain, offset, fc1_ref, fc2_ref):
    normed = jnp.concatenate([layer_norm(middle[at : at + 48], gain, offset).astype(BF)
                              for at in range(0, middle.shape[0], 48)], axis=0)
    total = None
    for j in range(4):
        v = jnp.dot(normed, fc1_ref[:, 512 * j : 512 * j + 512], preferred_element_type=F32)
        hidden = (v + v * lax.erf(v * (0.5 ** 0.5))).astype(BF)
        part = jnp.dot(hidden, fc2_ref[512 * j : 512 * j + 512, :], preferred_element_type=F32)
        total = part if total is None else total + part
    return middle + 0.5 * total


def block_masks(valid, first, n):
    t = lax.broadcasted_iota(jnp.int32, (n, 1), 0) + first
    u = lax.broadcasted_iota(jnp.int32, (1, WIN), 1)
    joint = jnp.where(t == u, 0.0, jnp.broadcast_to(valid, (n, WIN)))
    same = (t // QUART) % 2 == (u // QUART) % 2
    return joint, jnp.where(same, joint, NEG)


def put_block(block, gain, offset, normed_to=(), raw_to=()):
    levels = by_level(block)
    for pair in range(2):
        rows = jnp.concatenate([levels[level] for level in PAIRS[pair]], axis=0)
        normed = layer_norm(rows, gain, offset)
        for places, value in ((raw_to, rows), (normed_to, normed)):
            for ref, at, step in places:
                ref[pl.ds(pl.multiple_of(at + step * pair, 8), HALF), :] = value


def take_levels(from_ref, at, step):
    levels = [None] * LEV
    for pair in range(2):
        rows = from_ref[pl.ds(pl.multiple_of(at + step * pair, 8), HALF), :]
        for r in range(2):
            levels[PAIRS[pair][r]] = rows[QUART * r : QUART * r + QUART]
    return jnp.stack(levels)


def rest_of_block(rows, ctx_ref, xs_ref, proj_ref, g2_ref, b2_ref, fc1_ref, fc2_ref):
    moved = jnp.dot(ctx_ref[rows, :], proj_ref[...], preferred_element_type=F32).astype(BF)
    middle = xs_ref[rows, :] + moved.astype(F32)
    xs_ref[rows, :] = feed(middle, g2_ref[...], b2_ref[...], fc1_ref, fc2_ref)


def start_copies(pairs, sem):
    copies = [pltpu.make_async_copy(src, dst, sem.at[n]) for n, (src, dst) in enumerate(pairs)]
    for copy in copies:
        copy.start()
    return copies


Q_SCALE = HEAD_DIM ** -0.5 * LOG2E


def inner_kernel(tok_hbm, qkv_hbm, bias_hbm, proj_hbm, fc1_hbm, fc2_hbm, g1_ref, b1_ref, valid_ref, g2_ref, b2_ref,
                 out_hbm, tok_ref, qkv_ref, bias_ref, proj_ref, fc1_ref, fc2_ref, out_ref, xs_ref, q_ref,
                 kv_ref, ctx_ref, sem, out_sem):
    steps = tok_ref.shape[0] // WLAT
    inner = (pl.ds(SLAT, WLAT * steps), pl.ds(SLON, WLON))
    copies = start_copies([(tok_hbm.at[inner], tok_ref), (qkv_hbm, qkv_ref), (bias_hbm, bias_ref),
                           (proj_hbm, proj_ref), (fc1_hbm, fc1_ref), (fc2_hbm, fc2_ref)], sem)
    big = 2 * WIN
    part = big * steps // 2

    copies[0].wait()

    def load(i, carry):
        at = pl.multiple_of(big * i, big)
        x = tok_ref[pl.ds(WLAT * i, WLAT)]
        for h in range(2):
            put_block(x[:, 6 * h : 6 * h + 6], g1_ref[...], b1_ref[...], [(q_ref, at + HALF * h, WIN)],
                      [(xs_ref, at + HALF * h, WIN)])
        return carry

    lax.fori_loop(0, steps, load, 0)
    copies[1].wait()

    def project(i, carry):
        rows = pl.ds(pl.multiple_of(part * i, 16), part)
        normed = q_ref[rows, :].astype(BF)
        q_ref[rows, :] = jnp.dot(normed, qkv_ref[:, :C], preferred_element_type=F32) * Q_SCALE
        kv_ref[rows, :] = jnp.dot(normed, qkv_ref[:, C:], preferred_element_type=F32).astype(BF)
        return carry

    lax.fori_loop(0, 2, project, 0)
    copies[2].wait()

    def attention(i, carry):
        masks = block_masks(valid_ref[3 * (i + 1) + 1], 0, WIN)
        for pair in range(2):
            rows = pl.ds(pl.multiple_of(big * i + WIN * pair, WIN), WIN)
            ctx_ref[rows, :] = attend(q_ref[rows, :], kv_ref[rows, :C], kv_ref[rows, C:],
                                      lambda h: bias_ref[h], masks[pair]).astype(BF)
        return carry

    lax.fori_loop(0, steps, attention, 0)
    for copy in copies[3:]:
        copy.wait()

    def rest(i, carry):
        rest_of_block(pl.ds(pl.multiple_of(part * i, 16), part), ctx_ref, xs_ref, proj_ref, g2_ref, b2_ref,
                      fc1_ref, fc2_ref)
        return carry

    lax.fori_loop(0, 2, rest, 0)

    def out_copy(i):
        return pltpu.make_async_copy(out_ref.at[pl.ds(WLAT * i, WLAT)],
                                     out_hbm.at[pl.ds(SLAT + WLAT * i, WLAT), pl.ds(SLON, WLON)], out_sem.at[i])

    def store(i, carry):
        for h in range(2):
            levels = take_levels(xs_ref, pl.multiple_of(big * i, big) + HALF * h, WIN)
            out_ref[pl.ds(WLAT * i, WLAT), 6 * h : 6 * h + 6] = from_level(levels, (WLAT, 6, LEV, C))
        out_copy(i).start()
        return carry

    lax.fori_loop(0, steps, store, 0)
    for i in range(steps):
        out_copy(i).wait()


def edge_kernel(part_hbm, tok_hbm, west_hbm, east_hbm, north_hbm, south_hbm, qkv_hbm, bias1_hbm, bias2_hbm, proj_hbm,
                fc1_hbm, fc2_hbm, g1_ref, b1_ref, valid_ref, g2_ref, b2_ref, out_hbm,
                own_ref, strip_ref, west_ref, east_ref, north_ref, south_ref, qkv_ref, bias1_ref, bias2_ref, proj_ref,
                fc1_ref, fc2_ref, xs_ref, q_ref, kv_ref, ctx_ref, mid_ref, sem, out_sem):
    del part_hbm
    rows, cols = tok_hbm.shape[:2]
    steps = (rows - WLAT) // WLAT
    side_at = ((pl.ds(SLAT, WLAT * steps), pl.ds(0, SLON)), (pl.ds(SLAT, WLAT * steps), pl.ds(cols - SLON, SLON)))
    strip_at = (pl.ds(0, SLAT), pl.ds(rows - SLAT, SLAT))
    places = [(own_ref.at[side], side_at[side]) for side in range(2)]
    places += [(strip_ref.at[which], strip_at[which]) for which in range(2)]
    copies = start_copies([(tok_hbm.at[at], here) for here, at in places[:2]] + [
        (west_hbm, west_ref), (east_hbm, east_ref), (qkv_hbm, qkv_ref), (bias1_hbm, bias1_ref)] + [
        (tok_hbm.at[at], here) for here, at in places[2:]] + [
        (north_hbm, north_ref), (south_hbm, south_ref), (bias2_hbm, bias2_ref), (proj_hbm, proj_ref),
        (fc1_hbm, fc1_ref), (fc2_hbm, fc2_ref)], sem)
    big = 2 * WIN

    for copy in copies[:6]:
        copy.wait()

    def sides(i, carry):
        at = pl.multiple_of(big * i, big)
        own_rows, halo_rows = pl.ds(WLAT * i, WLAT), pl.ds(2 * SLAT + WLAT * i, WLAT)
        for side, halo_ref in ((0, west_ref), (1, east_ref)):
            put_block(own_ref[side, own_rows], g1_ref[...], b1_ref[...],
                      [(xs_ref, big * side + (HALF if side == 0 else 0), WIN)], [(mid_ref, at + WIN * side, HALF)])
            put_block(halo_ref[halo_rows], g1_ref[...], b1_ref[...],
                      [(xs_ref, big * side + (0 if side == 0 else HALF), WIN)])
        kv_ref[: 2 * big, :] = jnp.dot(xs_ref[: 2 * big, :].astype(BF), qkv_ref[:, C:],
                                       preferred_element_type=F32).astype(BF)
        own = jnp.concatenate([xs_ref[at : at + HALF, :] for at in (HALF, WIN + HALF, big, big + WIN)], axis=0)
        q_ref[...] = jnp.dot(own.astype(BF), qkv_ref[:, :C], preferred_element_type=F32) * Q_SCALE
        contexts = []
        for side in range(2):
            first = HALF if side == 0 else 0
            masks = block_masks(valid_ref[3 * (i + 1) + 2 * side], first, HALF)
            for pair in range(2):
                mine, keys = WIN * side + HALF * pair, big * side + WIN * pair
                contexts.append(attend(q_ref[mine : mine + HALF, :], kv_ref[keys : keys + WIN, :C],
                                       kv_ref[keys : keys + WIN, C:],
                                       lambda h: bias1_ref[h, first : first + HALF, :], masks[pair]))
        ctx_ref[pl.ds(at, big), :] = jnp.concatenate(contexts, axis=0).astype(BF)
        return carry

    lax.fori_loop(0, steps, sides, 0)
    for copy in copies[6:11]:
        copy.wait()

    for which in range(2):
        at = big * (steps + which)
        first = HALF if which == 0 else 0
        inside = slice(SLAT, 2 * SLAT) if which == 0 else slice(rows, rows + SLAT)
        outside = slice(0, SLAT) if which == 0 else slice(rows + SLAT, rows + 2 * SLAT)
        near_ref = (north_ref, south_ref)[which]
        own = jnp.concatenate([west_ref[inside], strip_ref[which], east_ref[inside]], axis=1)
        halo = jnp.concatenate([west_ref[outside], near_ref[...], east_ref[outside]], axis=1)
        for k in range(3):
            window = slice(WLON * k, WLON * k + WLON)
            mid = k == 1
            put_block(own[:, window], g1_ref[...], b1_ref[...],
                      [(xs_ref, big * k + first, WIN)] + ([(q_ref, 0, HALF)] if mid else []),
                      [(mid_ref, at, HALF)] if mid else [])
            put_block(halo[:, window], g1_ref[...], b1_ref[...], [(xs_ref, big * k + HALF - first, WIN)])
        corner = jnp.concatenate([strip_ref[which, :, cols - SLON :], strip_ref[which, :, :SLON]], axis=1)
        put_block(corner, g1_ref[...], b1_ref[...], [(q_ref, WIN, HALF)], [(mid_ref, at + WIN, HALF)])
        kv_ref[...] = jnp.dot(xs_ref[...].astype(BF), qkv_ref[:, C:], preferred_element_type=F32).astype(BF)
        q_ref[...] = jnp.dot(q_ref[...].astype(BF), qkv_ref[:, :C], preferred_element_type=F32) * Q_SCALE
        contexts = {}
        for k in range(3):
            masks = block_masks(valid_ref[18 * which + k], first, HALF)
            for pair in range(2):
                mine, keys = (0 if k == 1 else WIN) + HALF * pair, big * k + WIN * pair
                contexts[k, pair] = attend(q_ref[mine : mine + HALF, :], kv_ref[keys : keys + WIN, :C],
                                           kv_ref[keys : keys + WIN, C:],
                                           lambda h: bias2_ref[h, first : first + HALF, :], masks[pair])
        east_cell = lax.broadcasted_iota(jnp.int32, (HALF, 1), 0) % WLON < SLON
        ctx_ref[at : at + big, :] = jnp.concatenate(
            [contexts[1, 0], contexts[1, 1]] + [jnp.where(east_cell, contexts[2, pair], contexts[0, pair])
                                                for pair in range(2)], axis=0).astype(BF)
    for copy in copies[11:]:
        copy.wait()
    part = big * (steps + 2) // 3

    def rest(i, carry):
        rest_of_block(pl.ds(pl.multiple_of(part * i, 16), part), ctx_ref, mid_ref, proj_ref, g2_ref, b2_ref,
                      fc1_ref, fc2_ref)
        return carry

    lax.fori_loop(0, 3, rest, 0)

    def side_copy(i, side):
        return pltpu.make_async_copy(
            own_ref.at[side, pl.ds(WLAT * i, WLAT)],
            out_hbm.at[pl.ds(SLAT + WLAT * i, WLAT), pl.ds(side * (cols - SLON), SLON)], out_sem.at[2 * i + side])

    def store(i, carry):
        at = pl.multiple_of(big * i, big)
        for side in range(2):
            block = from_level(take_levels(mid_ref, at + WIN * side, HALF), (WLAT, SLON, LEV, C))
            own_ref[side, pl.ds(WLAT * i, WLAT)] = block
            side_copy(i, side).start()
        return carry

    lax.fori_loop(0, steps, store, 0)
    outs = []
    for which in range(2):
        at = big * (steps + which)
        strip_ref[which, :, SLON : SLON + WLON] = from_level(take_levels(mid_ref, at, HALF), (SLAT, WLON, LEV, C))
        block = from_level(take_levels(mid_ref, at + WIN, HALF), (SLAT, WLON, LEV, C))
        strip_ref[which, :, cols - SLON :] = block[:, :SLON]
        strip_ref[which, :, :SLON] = block[:, SLON:]
        outs.append(pltpu.make_async_copy(strip_ref.at[which], out_hbm.at[strip_at[which]],
                                          out_sem.at[2 * steps + which]))
        outs[-1].start()
    for i in range(steps):
        for side in range(2):
            side_copy(i, side).wait()
    for copy in outs:
        copy.wait()


def passed_along(block, axis, distance):
    size = lax.axis_size(axis)
    return lax.ppermute(block, axis, [((i - distance) % size, i) for i in range(size)])


def per_device(tokens, norm1_gain, norm1_bias, qkv_weight, rel_bias, key_mask, proj_weight,
               norm2_gain, norm2_bias, fc1_weight, fc2_weight):
    rows, cols = tokens.shape[:2]
    north = passed_along(tokens[rows - SLAT :], "lat", 1)
    south = passed_along(tokens[:SLAT], "lat", -1)

    vmem = pl.BlockSpec(memory_space=pltpu.VMEM)
    any_space = pl.BlockSpec(memory_space=pl.ANY)
    params = pltpu.CompilerParams(vmem_limit_bytes=VMEM_LIMIT)
    shape = (*key_mask.shape, rows, cols)
    bias1, bias2, valid = pl.pallas_call(
        functools.partial(prep_kernel, shape=shape),
        out_shape=[jax.ShapeDtypeStruct((HEADS, WIN, WIN), F32)] * 2 + [jax.ShapeDtypeStruct((21, 1, WIN), F32)],
        in_specs=[vmem, vmem],
        out_specs=[vmem] * 3,
        scratch_shapes=[pltpu.VMEM((HEADS, 768), F32), pltpu.VMEM((8 * WIN, 384), F32)],
        compiler_params=pltpu.CompilerParams(vmem_limit_bytes=56 * 1024 * 1024),
        cost_estimate=pl.CostEstimate(flops=10**9, bytes_accessed=5 * 10**6, transcendentals=0),
        name="prep",
    )(rel_bias, key_mask)

    def column(at):
        return jnp.concatenate([north[:, at], tokens[:, at], south[:, at]], axis=0)

    west = passed_along(column(slice(cols - SLON, cols)), "lon", 1)
    east = passed_along(column(slice(0, SLON)), "lon", -1)

    g1, b1 = norm1_gain.reshape(1, C), norm1_bias.reshape(1, C)
    g2, b2 = norm2_gain.reshape(1, C), norm2_bias.reshape(1, C)
    count = 2 * WIN * ((rows - WLAT) // WLAT)
    weights = [pltpu.VMEM((C, C), BF), pltpu.VMEM((C, FF), BF), pltpu.VMEM((FF, C), BF)]
    table_shape = pltpu.VMEM((HEADS, WIN, WIN), F32)
    inner_shape = pltpu.VMEM((rows - 2 * SLAT, WLON, LEV, C), BF)
    part = pl.pallas_call(
        inner_kernel,
        out_shape=jax.ShapeDtypeStruct(tokens.shape, BF),
        in_specs=[any_space] * 6 + [vmem] * 5,
        out_specs=any_space,
        scratch_shapes=[inner_shape, pltpu.VMEM((C, 3 * C), BF), table_shape, *weights, inner_shape,
                        pltpu.VMEM((count, C), F32), pltpu.VMEM((count, C), F32),
                        pltpu.VMEM((count, 2 * C), BF), pltpu.VMEM((count, C), BF),
                        pltpu.SemaphoreType.DMA((6,)), pltpu.SemaphoreType.DMA((count // (2 * WIN),))],
        compiler_params=params,
        cost_estimate=pl.CostEstimate(flops=12 * 10**9, bytes_accessed=12 * 10**6, transcendentals=0),
        name="inner",
    )(tokens, qkv_weight, bias1, proj_weight, fc1_weight, fc2_weight, g1, b1, valid, g2, b2)

    own = count + 4 * WIN
    strip = (SLAT, cols, LEV, C)
    halo = (rows + 2 * SLAT, SLON, LEV, C)
    return pl.pallas_call(
        edge_kernel,
        out_shape=jax.ShapeDtypeStruct(tokens.shape, BF),
        in_specs=[any_space] * 12 + [vmem] * 5,
        out_specs=any_space,
        scratch_shapes=[pltpu.VMEM((2, rows - 2 * SLAT, SLON, LEV, C), BF), pltpu.VMEM((2, *strip), BF),
                        pltpu.VMEM(halo, BF), pltpu.VMEM(halo, BF), pltpu.VMEM(strip, BF), pltpu.VMEM(strip, BF),
                        pltpu.VMEM((C, 3 * C), BF), table_shape, table_shape, *weights,
                        pltpu.VMEM((6 * WIN, C), F32), pltpu.VMEM((2 * WIN, C), F32), pltpu.VMEM((6 * WIN, 2 * C), BF),
                        pltpu.VMEM((own, C), BF), pltpu.VMEM((own, C), F32),
                        pltpu.SemaphoreType.DMA((14,)), pltpu.SemaphoreType.DMA((own // WIN,))],
        input_output_aliases={0: 0},
        compiler_params=params,
        cost_estimate=pl.CostEstimate(flops=16 * 10**9, bytes_accessed=16 * 10**6, transcendentals=0),
        name="edge",
    )(part, tokens, west, east, north, south, qkv_weight, bias1, bias2, proj_weight, fc1_weight, fc2_weight,
      g1, b1, valid, g2, b2)


def solution(mesh):
    return jax.shard_map(
        per_device,
        mesh=mesh,
        in_specs=(P("lat", "lon", None, None),) + (P(),) * 10,
        out_specs=P("lat", "lon", None, None),
        check_vma=False,
    )
```

```python
import functools
import math

import jax
import jax.numpy as jnp
import numpy as np
from jax import lax
from jax.experimental import pallas as pl
from jax.experimental.pallas import tpu as pltpu
from jax.sharding import PartitionSpec as P

C = 512
FF = 2048
HEADS = 8
HEAD_DIM = 64
WLEV = 2
WLAT = 6
WLON = 12
LEV = 4
SLAT = 3
SLON = 6
WIN = WLAT * WLON * WLEV
HALF = WIN // 2
QUART = WIN // 4
EPS = 1e-5
LOG2E = math.log2(math.e)
NEG = -jnp.inf
BF = jnp.bfloat16
F32 = jnp.float32
PAIRS = ((1, 2), (3, 0))
VMEM_LIMIT = 44 * 1024 * 1024


def order_columns():
    first = [(p, 6 * h + q, r) for h in range(2) for r in range(2) for p in range(6) for q in range(6)]
    second = [(3 * h + p, q, r) for h in range(2) for r in range(2) for p in range(3) for q in range(12)]
    return first, second


def lane_pqr(u, which):
    half, r, cell = u // HALF, (u // QUART) % 2, u % QUART
    if which == 0:
        return cell // 6, 6 * half + cell % 6, r
    return 3 * half + cell // 12, cell % 12, r


def prep_kernel(table_ref, mask_ref, bias1_ref, bias2_ref, valid_ref, wide_ref, rows_ref, *, shape):
    nlat, nlon, tile_rows, tile_cols = shape
    lat, lon, lats = lax.axis_index("lat"), lax.axis_index("lon"), nlat // tile_rows
    first, second = order_columns()
    wide_ref[...] = jnp.zeros_like(wide_ref)
    wide_ref[:, : table_ref.shape[1]] = table_ref[...] * LOG2E
    for t, (p, q, r) in enumerate(first):
        start = p * 69 + q * 3 + r
        rows_ref[8 * t : 8 * t + 8, :] = wide_ref[:, start : start + 384]
    rows = rows_ref[...]
    high = rows.astype(BF)
    low = (rows - high.astype(F32)).astype(BF)
    k = lax.broadcasted_iota(jnp.int32, (384, WIN), 0)
    for which, out_ref in enumerate((bias1_ref, bias2_ref)):
        p, q, r = lane_pqr(lax.broadcasted_iota(jnp.int32, (1, WIN), 1), which)
        pick = jnp.where(k == 379 - (p * 69 + q * 3 + r), 1.0, 0.0).astype(BF)
        full = jnp.dot(high, pick, preferred_element_type=F32) + jnp.dot(low, pick, preferred_element_type=F32)
        full = full.reshape(WIN, HEADS, WIN)
        if which == 1:
            full = jnp.stack([full[first.index(pqr)] for pqr in second])
        out_ref[...] = jnp.transpose(full, (1, 0, 2))
    row = lax.broadcasted_iota(jnp.int32, (48, 1), 0)
    col = lax.broadcasted_iota(jnp.int32, (48, nlat), 1)
    want = lax.rem(lat * tile_rows - SLAT + row + nlat, nlat)
    pick_rows = jnp.where(want == col, 1.0, 0.0).astype(BF)
    mask = (mask_ref[...] > 0).astype(F32).astype(BF)
    picked = jnp.dot(pick_rows, mask, preferred_element_type=F32).astype(BF)
    row = lax.broadcasted_iota(jnp.int32, (nlon, 3 * WIN), 0)
    row48 = lax.broadcasted_iota(jnp.int32, (48, 3 * WIN), 0)
    lane = lax.broadcasted_iota(jnp.int32, (1, 3 * WIN), 1)
    for which in range(2):
        p, q, _ = lane_pqr(lane % WIN, which)
        want = lax.rem(lon * tile_cols - SLON + 12 * (lane // WIN) + q + nlon, nlon)
        pick_cols = jnp.where(want == row, 1.0, 0.0).astype(BF)
        spread = jnp.dot(picked, pick_cols, preferred_element_type=F32)
        for window in (range(1, 6) if which == 0 else (0, 6)):
            value = jnp.sum(jnp.where(row48 == 6 * window + p, spread, 0.0), axis=0, keepdims=True)
            ok = value > 0.5
            if window == 0:
                ok = ok & ((lat > 0) | (lane % WIN >= HALF))
            if window == 6:
                ok = ok & ((lat < lats - 1) | (lane % WIN < HALF))
            value = jnp.where(ok, 0.0, NEG)
            for n in range(3):
                valid_ref[3 * window + n] = value[:, n * WIN : (n + 1) * WIN]


def layer_norm(values, gain, offset):
    average = jnp.mean(values, axis=-1, keepdims=True)
    centred = values - average
    spread = jnp.mean(centred * centred, axis=-1, keepdims=True)
    return centred * lax.rsqrt(spread + EPS) * gain + offset


def by_level(block):
    cells = block.astype(F32).reshape(QUART, LEV, C)
    return jnp.transpose(cells, (1, 0, 2))


def from_level(rows, shape):
    return jnp.transpose(rows, (1, 0, 2)).reshape(shape).astype(BF)


def attend(q, k, v, bias_of, block_mask):
    n = q.shape[0]
    head_of = lax.broadcasted_iota(jnp.int32, (1, 2 * HEAD_DIM), 1) // HEAD_DIM
    ones = jnp.ones((WIN, 2 * HEAD_DIM), BF)
    parts = []
    for g in range(HEADS // 2):
        lanes = slice(2 * HEAD_DIM * g, 2 * HEAD_DIM * (g + 1))
        qg = q[:, lanes]
        stacked = jnp.concatenate([jnp.where(head_of == j, qg, 0.0) for j in range(2)], axis=0).astype(BF)
        scores = lax.dot_general(stacked, k[:, lanes], (((1,), (1,)), ((), ())), preferred_element_type=F32)
        probs = []
        for j in range(2):
            s = scores[j * n : (j + 1) * n] + (bias_of(2 * g + j) + block_mask)
            probs.append(jnp.exp2(s - jnp.max(s, axis=-1, keepdims=True)))
        probs = jnp.concatenate(probs, axis=0).astype(BF)
        out = jnp.dot(probs, jnp.concatenate([v[:, lanes], ones], axis=1), preferred_element_type=F32)
        out = jnp.where(jnp.concatenate([head_of, head_of], axis=1) == 0, out[:n], out[n:])
        parts.append(out[:, : 2 * HEAD_DIM] / out[:, 2 * HEAD_DIM :])
    return jnp.concatenate(parts, axis=1)


def feed(middle, gain, offset, fc1_ref, fc2_ref):
    normed = jnp.concatenate([layer_norm(middle[at : at + 48], gain, offset).astype(BF)
                              for at in range(0, middle.shape[0], 48)], axis=0)
    total = None
    for j in range(4):
        v = jnp.dot(normed, fc1_ref[:, 512 * j : 512 * j + 512], preferred_element_type=F32)
        hidden = (v + v * lax.erf(v * (0.5 ** 0.5))).astype(BF)
        part = jnp.dot(hidden, fc2_ref[512 * j : 512 * j + 512, :], preferred_element_type=F32)
        total = part if total is None else total + part
    return middle + 0.5 * total


def block_masks(valid, first, n):
    t = lax.broadcasted_iota(jnp.int32, (n, 1), 0) + first
    u = lax.broadcasted_iota(jnp.int32, (1, WIN), 1)
    joint = jnp.where(t == u, 0.0, jnp.broadcast_to(valid, (n, WIN)))
    same = (t // QUART) % 2 == (u // QUART) % 2
    return joint, jnp.where(same, joint, NEG)


def put_block(block, gain, offset, normed_to=(), raw_to=()):
    levels = by_level(block)
    for pair in range(2):
        rows = jnp.concatenate([levels[level] for level in PAIRS[pair]], axis=0)
        normed = layer_norm(rows, gain, offset)
        for places, value in ((raw_to, rows), (normed_to, normed)):
            for ref, at, step in places:
                ref[pl.ds(pl.multiple_of(at + step * pair, 8), HALF), :] = value


def take_levels(from_ref, at, step):
    levels = [None] * LEV
    for pair in range(2):
        rows = from_ref[pl.ds(pl.multiple_of(at + step * pair, 8), HALF), :]
        for r in range(2):
            levels[PAIRS[pair][r]] = rows[QUART * r : QUART * r + QUART]
    return jnp.stack(levels)


def rest_of_block(rows, ctx_ref, xs_ref, proj_ref, g2_ref, b2_ref, fc1_ref, fc2_ref):
    moved = jnp.dot(ctx_ref[rows, :], proj_ref[...], preferred_element_type=F32).astype(BF)
    middle = xs_ref[rows, :] + moved.astype(F32)
    xs_ref[rows, :] = feed(middle, g2_ref[...], b2_ref[...], fc1_ref, fc2_ref)


def start_copies(pairs, sem):
    copies = [pltpu.make_async_copy(src, dst, sem.at[n]) for n, (src, dst) in enumerate(pairs)]
    for copy in copies:
        copy.start()
    return copies


Q_SCALE = HEAD_DIM ** -0.5 * LOG2E


def inner_kernel(tok_hbm, qkv_hbm, bias_hbm, proj_hbm, fc1_hbm, fc2_hbm, g1_ref, b1_ref, valid_ref, g2_ref, b2_ref,
                 out_hbm, tok_ref, qkv_ref, bias_ref, proj_ref, fc1_ref, fc2_ref, out_ref, xs_ref, q_ref,
                 kv_ref, ctx_ref, sem, out_sem):
    steps = tok_ref.shape[0] // WLAT
    inner = (pl.ds(SLAT, WLAT * steps), pl.ds(SLON, WLON))
    copies = start_copies([(tok_hbm.at[inner], tok_ref), (qkv_hbm, qkv_ref), (bias_hbm, bias_ref),
                           (proj_hbm, proj_ref), (fc1_hbm, fc1_ref), (fc2_hbm, fc2_ref)], sem)
    big = 2 * WIN
    part = big * steps // 2

    copies[0].wait()

    def load(i):
        at = pl.multiple_of(big * i, big)
        x = tok_ref[pl.ds(WLAT * i, WLAT)]
        for h in range(2):
            put_block(x[:, 6 * h : 6 * h + 6], g1_ref[...], b1_ref[...], [(q_ref, at + HALF * h, WIN)],
                      [(xs_ref, at + HALF * h, WIN)])

    for i in range(steps):
        load(i)
    copies[1].wait()

    def project(i, carry):
        rows = pl.ds(pl.multiple_of(part * i, 16), part)
        normed = q_ref[rows, :].astype(BF)
        q_ref[rows, :] = jnp.dot(normed, qkv_ref[:, :C], preferred_element_type=F32) * Q_SCALE
        kv_ref[rows, :] = jnp.dot(normed, qkv_ref[:, C:], preferred_element_type=F32).astype(BF)
        return carry

    lax.fori_loop(0, 2, project, 0)
    copies[2].wait()

    def attention(i):
        masks = block_masks(valid_ref[3 * (i + 1) + 1], 0, WIN)
        for pair in range(2):
            rows = pl.ds(pl.multiple_of(big * i + WIN * pair, WIN), WIN)
            ctx_ref[rows, :] = attend(q_ref[rows, :], kv_ref[rows, :C], kv_ref[rows, C:],
                                      lambda h: bias_ref[h], masks[pair]).astype(BF)

    for i in range(steps):
        attention(i)
    for copy in copies[3:]:
        copy.wait()

    def rest(i, carry):
        rest_of_block(pl.ds(pl.multiple_of(part * i, 16), part), ctx_ref, xs_ref, proj_ref, g2_ref, b2_ref,
                      fc1_ref, fc2_ref)
        return carry

    lax.fori_loop(0, 2, rest, 0)

    def out_copy(i):
        return pltpu.make_async_copy(out_ref.at[pl.ds(WLAT * i, WLAT)],
                                     out_hbm.at[pl.ds(SLAT + WLAT * i, WLAT), pl.ds(SLON, WLON)], out_sem.at[i])

    def store(i, carry):
        for h in range(2):
            levels = take_levels(xs_ref, pl.multiple_of(big * i, big) + HALF * h, WIN)
            out_ref[pl.ds(WLAT * i, WLAT), 6 * h : 6 * h + 6] = from_level(levels, (WLAT, 6, LEV, C))
        out_copy(i).start()
        return carry

    lax.fori_loop(0, steps, store, 0)
    for i in range(steps):
        out_copy(i).wait()


def edge_kernel(part_hbm, tok_hbm, west_hbm, east_hbm, north_hbm, south_hbm, qkv_hbm, bias1_hbm, bias2_hbm, proj_hbm,
                fc1_hbm, fc2_hbm, g1_ref, b1_ref, valid_ref, g2_ref, b2_ref, out_hbm,
                own_ref, strip_ref, west_ref, east_ref, north_ref, south_ref, qkv_ref, bias1_ref, bias2_ref, proj_ref,
                fc1_ref, fc2_ref, xs_ref, q_ref, kv_ref, ctx_ref, mid_ref, sem, out_sem):
    del part_hbm
    rows, cols = tok_hbm.shape[:2]
    steps = (rows - WLAT) // WLAT
    side_at = ((pl.ds(SLAT, WLAT * steps), pl.ds(0, SLON)), (pl.ds(SLAT, WLAT * steps), pl.ds(cols - SLON, SLON)))
    strip_at = (pl.ds(0, SLAT), pl.ds(rows - SLAT, SLAT))
    places = [(own_ref.at[side], side_at[side]) for side in range(2)]
    places += [(strip_ref.at[which], strip_at[which]) for which in range(2)]
    copies = start_copies([(tok_hbm.at[at], here) for here, at in places[:2]] + [
        (west_hbm, west_ref), (east_hbm, east_ref), (qkv_hbm, qkv_ref), (bias1_hbm, bias1_ref)] + [
        (tok_hbm.at[at], here) for here, at in places[2:]] + [
        (north_hbm, north_ref), (south_hbm, south_ref), (bias2_hbm, bias2_ref), (proj_hbm, proj_ref),
        (fc1_hbm, fc1_ref), (fc2_hbm, fc2_ref)], sem)
    big = 2 * WIN

    for copy in copies[:6]:
        copy.wait()

    def sides(i):
        at = big * i
        base, mine_base = 2 * big * (i % 2), big * (i % 2)
        own_rows, halo_rows = pl.ds(WLAT * i, WLAT), pl.ds(2 * SLAT + WLAT * i, WLAT)
        for side, halo_ref in ((0, west_ref), (1, east_ref)):
            here, there = (HALF, 0) if side == 0 else (0, HALF)
            put_block(own_ref[side, own_rows], g1_ref[...], b1_ref[...],
                      [(xs_ref, base + big * side + here, WIN)], [(mid_ref, at + WIN * side, HALF)])
            put_block(halo_ref[halo_rows], g1_ref[...], b1_ref[...], [(xs_ref, base + big * side + there, WIN)])
        keys_all = slice(base, base + 2 * big)
        kv_ref[keys_all, :] = jnp.dot(xs_ref[keys_all, :].astype(BF), qkv_ref[:, C:],
                                      preferred_element_type=F32).astype(BF)
        own = jnp.concatenate([xs_ref[base + row : base + row + HALF, :]
                               for row in (HALF, WIN + HALF, big, big + WIN)], axis=0)
        q_ref[mine_base : mine_base + big, :] = jnp.dot(own.astype(BF), qkv_ref[:, :C],
                                                        preferred_element_type=F32) * Q_SCALE
        contexts = []
        for side in range(2):
            first = HALF if side == 0 else 0
            masks = block_masks(valid_ref[3 * (i + 1) + 2 * side], first, HALF)
            for pair in range(2):
                mine, keys = mine_base + WIN * side + HALF * pair, base + big * side + WIN * pair
                contexts.append(attend(q_ref[mine : mine + HALF, :], kv_ref[keys : keys + WIN, :C],
                                       kv_ref[keys : keys + WIN, C:],
                                       lambda h: bias1_ref[h, first : first + HALF, :], masks[pair]))
        ctx_ref[at : at + big, :] = jnp.concatenate(contexts, axis=0).astype(BF)

    for i in range(steps):
        sides(i)
    for copy in copies[6:11]:
        copy.wait()

    for which in range(2):
        at = big * (steps + which)
        first = HALF if which == 0 else 0
        inside = slice(SLAT, 2 * SLAT) if which == 0 else slice(rows, rows + SLAT)
        outside = slice(0, SLAT) if which == 0 else slice(rows + SLAT, rows + 2 * SLAT)
        near_ref = (north_ref, south_ref)[which]
        own = jnp.concatenate([west_ref[inside], strip_ref[which], east_ref[inside]], axis=1)
        halo = jnp.concatenate([west_ref[outside], near_ref[...], east_ref[outside]], axis=1)
        for k in range(3):
            window = slice(WLON * k, WLON * k + WLON)
            mid = k == 1
            put_block(own[:, window], g1_ref[...], b1_ref[...],
                      [(xs_ref, big * k + first, WIN)] + ([(q_ref, 0, HALF)] if mid else []),
                      [(mid_ref, at, HALF)] if mid else [])
            put_block(halo[:, window], g1_ref[...], b1_ref[...], [(xs_ref, big * k + HALF - first, WIN)])
        corner = jnp.concatenate([strip_ref[which, :, cols - SLON :], strip_ref[which, :, :SLON]], axis=1)
        put_block(corner, g1_ref[...], b1_ref[...], [(q_ref, WIN, HALF)], [(mid_ref, at + WIN, HALF)])
        kv_ref[: 3 * big, :] = jnp.dot(xs_ref[: 3 * big, :].astype(BF), qkv_ref[:, C:],
                                       preferred_element_type=F32).astype(BF)
        q_ref[:big, :] = jnp.dot(q_ref[:big, :].astype(BF), qkv_ref[:, :C], preferred_element_type=F32) * Q_SCALE
        contexts = {}
        for k in range(3):
            masks = block_masks(valid_ref[18 * which + k], first, HALF)
            for pair in range(2):
                mine, keys = (0 if k == 1 else WIN) + HALF * pair, big * k + WIN * pair
                contexts[k, pair] = attend(q_ref[mine : mine + HALF, :], kv_ref[keys : keys + WIN, :C],
                                           kv_ref[keys : keys + WIN, C:],
                                           lambda h: bias2_ref[h, first : first + HALF, :], masks[pair])
        east_cell = lax.broadcasted_iota(jnp.int32, (HALF, 1), 0) % WLON < SLON
        ctx_ref[at : at + big, :] = jnp.concatenate(
            [contexts[1, 0], contexts[1, 1]] + [jnp.where(east_cell, contexts[2, pair], contexts[0, pair])
                                                for pair in range(2)], axis=0).astype(BF)
    for copy in copies[11:]:
        copy.wait()
    part = big * (steps + 2) // 3

    def rest(i, carry):
        rest_of_block(pl.ds(pl.multiple_of(part * i, 16), part), ctx_ref, mid_ref, proj_ref, g2_ref, b2_ref,
                      fc1_ref, fc2_ref)
        return carry

    lax.fori_loop(0, 3, rest, 0)

    def side_copy(i, side):
        return pltpu.make_async_copy(
            own_ref.at[side, pl.ds(WLAT * i, WLAT)],
            out_hbm.at[pl.ds(SLAT + WLAT * i, WLAT), pl.ds(side * (cols - SLON), SLON)], out_sem.at[2 * i + side])

    def store(i, carry):
        at = pl.multiple_of(big * i, big)
        for side in range(2):
            block = from_level(take_levels(mid_ref, at + WIN * side, HALF), (WLAT, SLON, LEV, C))
            own_ref[side, pl.ds(WLAT * i, WLAT)] = block
            side_copy(i, side).start()
        return carry

    lax.fori_loop(0, steps, store, 0)
    outs = []
    for which in range(2):
        at = big * (steps + which)
        strip_ref[which, :, SLON : SLON + WLON] = from_level(take_levels(mid_ref, at, HALF), (SLAT, WLON, LEV, C))
        block = from_level(take_levels(mid_ref, at + WIN, HALF), (SLAT, WLON, LEV, C))
        strip_ref[which, :, cols - SLON :] = block[:, :SLON]
        strip_ref[which, :, :SLON] = block[:, SLON:]
        outs.append(pltpu.make_async_copy(strip_ref.at[which], out_hbm.at[strip_at[which]],
                                          out_sem.at[2 * steps + which]))
        outs[-1].start()
    for i in range(steps):
        for side in range(2):
            side_copy(i, side).wait()
    for copy in outs:
        copy.wait()


def passed_along(block, axis, distance):
    size = lax.axis_size(axis)
    return lax.ppermute(block, axis, [((i - distance) % size, i) for i in range(size)])


def per_device(tokens, norm1_gain, norm1_bias, qkv_weight, rel_bias, key_mask, proj_weight,
               norm2_gain, norm2_bias, fc1_weight, fc2_weight):
    rows, cols = tokens.shape[:2]
    north = passed_along(tokens[rows - SLAT :], "lat", 1)
    south = passed_along(tokens[:SLAT], "lat", -1)

    vmem = pl.BlockSpec(memory_space=pltpu.VMEM)
    any_space = pl.BlockSpec(memory_space=pl.ANY)
    params = pltpu.CompilerParams(vmem_limit_bytes=VMEM_LIMIT)
    shape = (*key_mask.shape, rows, cols)
    bias1, bias2, valid = pl.pallas_call(
        functools.partial(prep_kernel, shape=shape),
        out_shape=[jax.ShapeDtypeStruct((HEADS, WIN, WIN), F32)] * 2 + [jax.ShapeDtypeStruct((21, 1, WIN), F32)],
        in_specs=[vmem, vmem],
        out_specs=[vmem] * 3,
        scratch_shapes=[pltpu.VMEM((HEADS, 768), F32), pltpu.VMEM((8 * WIN, 384), F32)],
        compiler_params=pltpu.CompilerParams(vmem_limit_bytes=40 * 1024 * 1024),
        cost_estimate=pl.CostEstimate(flops=10**9, bytes_accessed=5 * 10**6, transcendentals=0),
        name="prep",
    )(rel_bias, key_mask)

    def column(at):
        return jnp.concatenate([north[:, at], tokens[:, at], south[:, at]], axis=0)

    west = passed_along(column(slice(cols - SLON, cols)), "lon", 1)
    east = passed_along(column(slice(0, SLON)), "lon", -1)

    g1, b1 = norm1_gain.reshape(1, C), norm1_bias.reshape(1, C)
    g2, b2 = norm2_gain.reshape(1, C), norm2_bias.reshape(1, C)
    count = 2 * WIN * ((rows - WLAT) // WLAT)
    weights = [pltpu.VMEM((C, C), BF), pltpu.VMEM((C, FF), BF), pltpu.VMEM((FF, C), BF)]
    table_shape = pltpu.VMEM((HEADS, WIN, WIN), F32)
    inner_shape = pltpu.VMEM((rows - 2 * SLAT, WLON, LEV, C), BF)
    part = pl.pallas_call(
        inner_kernel,
        out_shape=jax.ShapeDtypeStruct(tokens.shape, BF),
        in_specs=[any_space] * 6 + [vmem] * 5,
        out_specs=any_space,
        scratch_shapes=[inner_shape, pltpu.VMEM((C, 3 * C), BF), table_shape, *weights, inner_shape,
                        pltpu.VMEM((count, C), F32), pltpu.VMEM((count, C), F32),
                        pltpu.VMEM((count, 2 * C), BF), pltpu.VMEM((count, C), BF),
                        pltpu.SemaphoreType.DMA((6,)), pltpu.SemaphoreType.DMA((count // (2 * WIN),))],
        compiler_params=params,
        cost_estimate=pl.CostEstimate(flops=12 * 10**9, bytes_accessed=12 * 10**6, transcendentals=0),
        name="inner",
    )(tokens, qkv_weight, bias1, proj_weight, fc1_weight, fc2_weight, g1, b1, valid, g2, b2)

    own = count + 4 * WIN
    strip = (SLAT, cols, LEV, C)
    halo = (rows + 2 * SLAT, SLON, LEV, C)
    return pl.pallas_call(
        edge_kernel,
        out_shape=jax.ShapeDtypeStruct(tokens.shape, BF),
        in_specs=[any_space] * 12 + [vmem] * 5,
        out_specs=any_space,
        scratch_shapes=[pltpu.VMEM((2, rows - 2 * SLAT, SLON, LEV, C), BF), pltpu.VMEM((2, *strip), BF),
                        pltpu.VMEM(halo, BF), pltpu.VMEM(halo, BF), pltpu.VMEM(strip, BF), pltpu.VMEM(strip, BF),
                        pltpu.VMEM((C, 3 * C), BF), table_shape, table_shape, *weights,
                        pltpu.VMEM((8 * WIN, C), F32), pltpu.VMEM((4 * WIN, C), F32), pltpu.VMEM((8 * WIN, 2 * C), BF),
                        pltpu.VMEM((own, C), BF), pltpu.VMEM((own, C), F32),
                        pltpu.SemaphoreType.DMA((14,)), pltpu.SemaphoreType.DMA((own // WIN,))],
        input_output_aliases={0: 0},
        compiler_params=params,
        cost_estimate=pl.CostEstimate(flops=16 * 10**9, bytes_accessed=16 * 10**6, transcendentals=0),
        name="edge",
    )(part, tokens, west, east, north, south, qkv_weight, bias1, bias2, proj_weight, fc1_weight, fc2_weight,
      g1, b1, valid, g2, b2)


def solution(mesh):
    return jax.shard_map(
        per_device,
        mesh=mesh,
        in_specs=(P("lat", "lon", None, None),) + (P(),) * 10,
        out_specs=P("lat", "lon", None, None),
        check_vma=False,
    )
```

```python
import functools
import math

import jax
import jax.numpy as jnp
import numpy as np
from jax import lax
from jax.experimental import pallas as pl
from jax.experimental.pallas import tpu as pltpu
from jax.sharding import PartitionSpec as P

C = 512
FF = 2048
HEADS = 8
HEAD_DIM = 64
WLEV = 2
WLAT = 6
WLON = 12
LEV = 4
SLAT = 3
SLON = 6
WIN = WLAT * WLON * WLEV
HALF = WIN // 2
QUART = WIN // 4
EPS = 1e-5
LOG2E = math.log2(math.e)
NEG = -jnp.inf
BF = jnp.bfloat16
F32 = jnp.float32
PAIRS = ((1, 2), (3, 0))
VMEM_LIMIT = 44 * 1024 * 1024


def order_columns():
    first = [(p, 6 * h + q, r) for h in range(2) for r in range(2) for p in range(6) for q in range(6)]
    second = [(3 * h + p, q, r) for h in range(2) for r in range(2) for p in range(3) for q in range(12)]
    return first, second


def lane_pqr(u, which):
    half, r, cell = u // HALF, (u // QUART) % 2, u % QUART
    if which == 0:
        return cell // 6, 6 * half + cell % 6, r
    return 3 * half + cell // 12, cell % 12, r


def prep_kernel(table_ref, mask_ref, bias1_ref, bias2_ref, valid_ref, wide_ref, rows_ref, *, shape):
    nlat, nlon, tile_rows, tile_cols = shape
    lat, lon, lats = lax.axis_index("lat"), lax.axis_index("lon"), nlat // tile_rows
    first, second = order_columns()
    wide_ref[...] = jnp.zeros_like(wide_ref)
    wide_ref[:, : table_ref.shape[1]] = table_ref[...] * LOG2E
    for t, (p, q, r) in enumerate(first):
        start = p * 69 + q * 3 + r
        rows_ref[8 * t : 8 * t + 8, :] = wide_ref[:, start : start + 384]
    rows = rows_ref[...]
    high = rows.astype(BF)
    low = (rows - high.astype(F32)).astype(BF)
    k = lax.broadcasted_iota(jnp.int32, (384, WIN), 0)
    for which, out_ref in enumerate((bias1_ref, bias2_ref)):
        p, q, r = lane_pqr(lax.broadcasted_iota(jnp.int32, (1, WIN), 1), which)
        pick = jnp.where(k == 379 - (p * 69 + q * 3 + r), 1.0, 0.0).astype(BF)
        full = jnp.dot(high, pick, preferred_element_type=F32) + jnp.dot(low, pick, preferred_element_type=F32)
        full = full.reshape(WIN, HEADS, WIN)
        if which == 1:
            full = jnp.stack([full[first.index(pqr)] for pqr in second])
        out_ref[...] = jnp.transpose(full, (1, 0, 2))
    row = lax.broadcasted_iota(jnp.int32, (48, 1), 0)
    col = lax.broadcasted_iota(jnp.int32, (48, nlat), 1)
    want = lax.rem(lat * tile_rows - SLAT + row + nlat, nlat)
    pick_rows = jnp.where(want == col, 1.0, 0.0).astype(BF)
    mask = (mask_ref[...] > 0).astype(F32).astype(BF)
    picked = jnp.dot(pick_rows, mask, preferred_element_type=F32).astype(BF)
    row = lax.broadcasted_iota(jnp.int32, (nlon, 3 * WIN), 0)
    row48 = lax.broadcasted_iota(jnp.int32, (48, 3 * WIN), 0)
    lane = lax.broadcasted_iota(jnp.int32, (1, 3 * WIN), 1)
    for which in range(2):
        p, q, _ = lane_pqr(lane % WIN, which)
        want = lax.rem(lon * tile_cols - SLON + 12 * (lane // WIN) + q + nlon, nlon)
        pick_cols = jnp.where(want == row, 1.0, 0.0).astype(BF)
        spread = jnp.dot(picked, pick_cols, preferred_element_type=F32)
        for window in (range(1, 6) if which == 0 else (0, 6)):
            value = jnp.sum(jnp.where(row48 == 6 * window + p, spread, 0.0), axis=0, keepdims=True)
            ok = value > 0.5
            if window == 0:
                ok = ok & ((lat > 0) | (lane % WIN >= HALF))
            if window == 6:
                ok = ok & ((lat < lats - 1) | (lane % WIN < HALF))
            value = jnp.where(ok, 0.0, NEG)
            for n in range(3):
                valid_ref[3 * window + n] = value[:, n * WIN : (n + 1) * WIN]


def layer_norm(values, gain, offset):
    average = jnp.mean(values, axis=-1, keepdims=True)
    centred = values - average
    spread = jnp.mean(centred * centred, axis=-1, keepdims=True)
    return centred * lax.rsqrt(spread + EPS) * gain + offset


def by_level(block):
    cells = block.astype(F32).reshape(QUART, LEV, C)
    return jnp.transpose(cells, (1, 0, 2))


def from_level(rows, shape):
    return jnp.transpose(rows, (1, 0, 2)).reshape(shape).astype(BF)


def attend(q, k, v, bias_of, block_mask):
    n = q.shape[0]
    head_of = lax.broadcasted_iota(jnp.int32, (1, 2 * HEAD_DIM), 1) // HEAD_DIM
    ones = jnp.ones((WIN, 2 * HEAD_DIM), BF)
    parts = []
    for g in range(HEADS // 2):
        lanes = slice(2 * HEAD_DIM * g, 2 * HEAD_DIM * (g + 1))
        qg = q[:, lanes]
        stacked = jnp.concatenate([jnp.where(head_of == j, qg, 0.0) for j in range(2)], axis=0).astype(BF)
        scores = lax.dot_general(stacked, k[:, lanes], (((1,), (1,)), ((), ())), preferred_element_type=F32)
        probs = []
        for j in range(2):
            s = scores[j * n : (j + 1) * n] + (bias_of(2 * g + j) + block_mask)
            probs.append(jnp.exp2(s - jnp.max(s, axis=-1, keepdims=True)))
        probs = jnp.concatenate(probs, axis=0).astype(BF)
        out = jnp.dot(probs, jnp.concatenate([v[:, lanes], ones], axis=1), preferred_element_type=F32)
        out = jnp.where(jnp.concatenate([head_of, head_of], axis=1) == 0, out[:n], out[n:])
        parts.append(out[:, : 2 * HEAD_DIM] / out[:, 2 * HEAD_DIM :])
    return jnp.concatenate(parts, axis=1)


def feed(middle, gain, offset, fc1_ref, fc2_ref):
    normed = jnp.concatenate([layer_norm(middle[at : at + 48], gain, offset).astype(BF)
                              for at in range(0, middle.shape[0], 48)], axis=0)
    total = None
    for j in range(4):
        v = jnp.dot(normed, fc1_ref[:, 512 * j : 512 * j + 512], preferred_element_type=F32)
        hidden = (v + v * lax.erf(v * (0.5 ** 0.5))).astype(BF)
        part = jnp.dot(hidden, fc2_ref[512 * j : 512 * j + 512, :], preferred_element_type=F32)
        total = part if total is None else total + part
    return middle + 0.5 * total


def block_masks(valid, first, n):
    t = lax.broadcasted_iota(jnp.int32, (n, 1), 0) + first
    u = lax.broadcasted_iota(jnp.int32, (1, WIN), 1)
    joint = jnp.where(t == u, 0.0, jnp.broadcast_to(valid, (n, WIN)))
    same = (t // QUART) % 2 == (u // QUART) % 2
    return joint, jnp.where(same, joint, NEG)


def put_block(block, gain, offset, normed_to=(), raw_to=()):
    levels = by_level(block)
    for pair in range(2):
        rows = jnp.concatenate([levels[level] for level in PAIRS[pair]], axis=0)
        normed = layer_norm(rows, gain, offset)
        for places, value in ((raw_to, rows), (normed_to, normed)):
            for ref, at, step in places:
                ref[pl.ds(pl.multiple_of(at + step * pair, 8), HALF), :] = value


def take_levels(from_ref, at, step):
    levels = [None] * LEV
    for pair in range(2):
        rows = from_ref[pl.ds(pl.multiple_of(at + step * pair, 8), HALF), :]
        for r in range(2):
            levels[PAIRS[pair][r]] = rows[QUART * r : QUART * r + QUART]
    return jnp.stack(levels)


def rest_of_block(rows, ctx_ref, xs_ref, proj_ref, g2_ref, b2_ref, fc1_ref, fc2_ref):
    moved = jnp.dot(ctx_ref[rows, :], proj_ref[...], preferred_element_type=F32).astype(BF)
    middle = xs_ref[rows, :] + moved.astype(F32)
    xs_ref[rows, :] = feed(middle, g2_ref[...], b2_ref[...], fc1_ref, fc2_ref)


def start_copies(pairs, sem):
    copies = [pltpu.make_async_copy(src, dst, sem.at[n]) for n, (src, dst) in enumerate(pairs)]
    for copy in copies:
        copy.start()
    return copies


Q_SCALE = HEAD_DIM ** -0.5 * LOG2E


def inner_kernel(tok_hbm, qkv_hbm, bias_hbm, proj_hbm, fc1_hbm, fc2_hbm, g1_ref, b1_ref, valid_ref, g2_ref, b2_ref,
                 out_hbm, tok_ref, qkv_ref, bias_ref, proj_ref, fc1_ref, fc2_ref, out_ref, xs_ref, q_ref,
                 kv_ref, ctx_ref, sem, out_sem):
    steps = tok_ref.shape[0] // WLAT
    inner = (pl.ds(SLAT, WLAT * steps), pl.ds(SLON, WLON))
    copies = start_copies([(tok_hbm.at[inner], tok_ref), (qkv_hbm, qkv_ref), (bias_hbm, bias_ref),
                           (proj_hbm, proj_ref), (fc1_hbm, fc1_ref), (fc2_hbm, fc2_ref)], sem)
    big = 2 * WIN
    part = big * steps // 2

    copies[0].wait()

    def load(i):
        at = pl.multiple_of(big * i, big)
        x = tok_ref[pl.ds(WLAT * i, WLAT)]
        for h in range(2):
            put_block(x[:, 6 * h : 6 * h + 6], g1_ref[...], b1_ref[...], [(q_ref, at + HALF * h, WIN)],
                      [(xs_ref, at + HALF * h, WIN)])

    for i in range(steps):
        load(i)
    copies[1].wait()

    def project(i, carry):
        rows = pl.ds(pl.multiple_of(part * i, 16), part)
        normed = q_ref[rows, :].astype(BF)
        q_ref[rows, :] = jnp.dot(normed, qkv_ref[:, :C], preferred_element_type=F32) * Q_SCALE
        kv_ref[rows, :] = jnp.dot(normed, qkv_ref[:, C:], preferred_element_type=F32).astype(BF)
        return carry

    lax.fori_loop(0, 2, project, 0)
    copies[2].wait()

    def attention(i):
        masks = block_masks(valid_ref[3 * (i + 1) + 1], 0, WIN)
        for pair in range(2):
            rows = pl.ds(pl.multiple_of(big * i + WIN * pair, WIN), WIN)
            ctx_ref[rows, :] = attend(q_ref[rows, :], kv_ref[rows, :C], kv_ref[rows, C:],
                                      lambda h: bias_ref[h], masks[pair]).astype(BF)

    for i in range(steps):
        attention(i)
    for copy in copies[3:]:
        copy.wait()

    def rest(i, carry):
        rest_of_block(pl.ds(pl.multiple_of(part * i, 16), part), ctx_ref, xs_ref, proj_ref, g2_ref, b2_ref,
                      fc1_ref, fc2_ref)
        return carry

    lax.fori_loop(0, 2, rest, 0)

    def out_copy(i):
        return pltpu.make_async_copy(out_ref.at[pl.ds(WLAT * i, WLAT)],
                                     out_hbm.at[pl.ds(SLAT + WLAT * i, WLAT), pl.ds(SLON, WLON)], out_sem.at[i])

    def store(i, carry):
        for h in range(2):
            levels = take_levels(xs_ref, pl.multiple_of(big * i, big) + HALF * h, WIN)
            out_ref[pl.ds(WLAT * i, WLAT), 6 * h : 6 * h + 6] = from_level(levels, (WLAT, 6, LEV, C))
        out_copy(i).start()
        return carry

    lax.fori_loop(0, steps, store, 0)
    for i in range(steps):
        out_copy(i).wait()


def edge_kernel(part_hbm, tok_hbm, west_hbm, east_hbm, north_hbm, south_hbm, west_ends_hbm, east_ends_hbm, qkv_hbm, bias1_hbm, bias2_hbm, proj_hbm,
                fc1_hbm, fc2_hbm, g1_ref, b1_ref, valid_ref, g2_ref, b2_ref, out_hbm,
                own_ref, strip_ref, west_ref, east_ref, north_ref, south_ref, qkv_ref, bias1_ref, bias2_ref, proj_ref,
                fc1_ref, fc2_ref, xs_ref, q_ref, kv_ref, ctx_ref, mid_ref, sem, out_sem):
    del part_hbm
    rows, cols = tok_hbm.shape[:2]
    steps = (rows - WLAT) // WLAT
    side_at = ((pl.ds(SLAT, WLAT * steps), pl.ds(0, SLON)), (pl.ds(SLAT, WLAT * steps), pl.ds(cols - SLON, SLON)))
    strip_at = (pl.ds(0, SLAT), pl.ds(rows - SLAT, SLAT))
    places = [(own_ref.at[side], side_at[side]) for side in range(2)]
    places += [(strip_ref.at[which], strip_at[which]) for which in range(2)]
    copies = start_copies([(tok_hbm.at[at], here) for here, at in places[:2]] + [
        (west_hbm, west_ref.at[pl.ds(SLAT, rows)]), (east_hbm, east_ref.at[pl.ds(SLAT, rows)]), (qkv_hbm, qkv_ref), (bias1_hbm, bias1_ref)] + [
        (tok_hbm.at[at], here) for here, at in places[2:]] + [
        (ends.at[pl.ds(SLAT * n, SLAT)], ref.at[pl.ds(at, SLAT)])
        for ends, ref in ((west_ends_hbm, west_ref), (east_ends_hbm, east_ref)) for n, at in ((0, 0), (1, rows + SLAT))] + [
        (north_hbm, north_ref), (south_hbm, south_ref), (bias2_hbm, bias2_ref), (proj_hbm, proj_ref),
        (fc1_hbm, fc1_ref), (fc2_hbm, fc2_ref)], sem)
    big = 2 * WIN

    for copy in copies[:6]:
        copy.wait()

    def sides(i):
        at = big * i
        base, mine_base = 2 * big * (i % 2), big * (i % 2)
        own_rows, halo_rows = pl.ds(WLAT * i, WLAT), pl.ds(2 * SLAT + WLAT * i, WLAT)
        for side, halo_ref in ((0, west_ref), (1, east_ref)):
            here, there = (HALF, 0) if side == 0 else (0, HALF)
            put_block(own_ref[side, own_rows], g1_ref[...], b1_ref[...],
                      [(xs_ref, base + big * side + here, WIN)], [(mid_ref, at + WIN * side, HALF)])
            put_block(halo_ref[halo_rows], g1_ref[...], b1_ref[...], [(xs_ref, base + big * side + there, WIN)])
        keys_all = slice(base, base + 2 * big)
        kv_ref[keys_all, :] = jnp.dot(xs_ref[keys_all, :].astype(BF), qkv_ref[:, C:],
                                      preferred_element_type=F32).astype(BF)
        own = jnp.concatenate([xs_ref[base + row : base + row + HALF, :]
                               for row in (HALF, WIN + HALF, big, big + WIN)], axis=0)
        q_ref[mine_base : mine_base + big, :] = jnp.dot(own.astype(BF), qkv_ref[:, :C],
                                                        preferred_element_type=F32) * Q_SCALE
        contexts = []
        for side in range(2):
            first = HALF if side == 0 else 0
            masks = block_masks(valid_ref[3 * (i + 1) + 2 * side], first, HALF)
            for pair in range(2):
                mine, keys = mine_base + WIN * side + HALF * pair, base + big * side + WIN * pair
                contexts.append(attend(q_ref[mine : mine + HALF, :], kv_ref[keys : keys + WIN, :C],
                                       kv_ref[keys : keys + WIN, C:],
                                       lambda h: bias1_ref[h, first : first + HALF, :], masks[pair]))
        ctx_ref[at : at + big, :] = jnp.concatenate(contexts, axis=0).astype(BF)

    for i in range(steps):
        sides(i)
    for copy in copies[6:15]:
        copy.wait()

    for which in range(2):
        at = big * (steps + which)
        first = HALF if which == 0 else 0
        inside = slice(SLAT, 2 * SLAT) if which == 0 else slice(rows, rows + SLAT)
        outside = slice(0, SLAT) if which == 0 else slice(rows + SLAT, rows + 2 * SLAT)
        near_ref = (north_ref, south_ref)[which]
        own = jnp.concatenate([west_ref[inside], strip_ref[which], east_ref[inside]], axis=1)
        halo = jnp.concatenate([west_ref[outside], near_ref[...], east_ref[outside]], axis=1)
        for k in range(3):
            window = slice(WLON * k, WLON * k + WLON)
            mid = k == 1
            put_block(own[:, window], g1_ref[...], b1_ref[...],
                      [(xs_ref, big * k + first, WIN)] + ([(q_ref, 0, HALF)] if mid else []),
                      [(mid_ref, at, HALF)] if mid else [])
            put_block(halo[:, window], g1_ref[...], b1_ref[...], [(xs_ref, big * k + HALF - first, WIN)])
        corner = jnp.concatenate([strip_ref[which, :, cols - SLON :], strip_ref[which, :, :SLON]], axis=1)
        put_block(corner, g1_ref[...], b1_ref[...], [(q_ref, WIN, HALF)], [(mid_ref, at + WIN, HALF)])
        kv_ref[: 3 * big, :] = jnp.dot(xs_ref[: 3 * big, :].astype(BF), qkv_ref[:, C:],
                                       preferred_element_type=F32).astype(BF)
        q_ref[:big, :] = jnp.dot(q_ref[:big, :].astype(BF), qkv_ref[:, :C], preferred_element_type=F32) * Q_SCALE
        contexts = {}
        for k in range(3):
            masks = block_masks(valid_ref[18 * which + k], first, HALF)
            for pair in range(2):
                mine, keys = (0 if k == 1 else WIN) + HALF * pair, big * k + WIN * pair
                contexts[k, pair] = attend(q_ref[mine : mine + HALF, :], kv_ref[keys : keys + WIN, :C],
                                           kv_ref[keys : keys + WIN, C:],
                                           lambda h: bias2_ref[h, first : first + HALF, :], masks[pair])
        east_cell = lax.broadcasted_iota(jnp.int32, (HALF, 1), 0) % WLON < SLON
        ctx_ref[at : at + big, :] = jnp.concatenate(
            [contexts[1, 0], contexts[1, 1]] + [jnp.where(east_cell, contexts[2, pair], contexts[0, pair])
                                                for pair in range(2)], axis=0).astype(BF)
    for copy in copies[15:]:
        copy.wait()
    part = big * (steps + 2) // 3

    def rest(i, carry):
        rest_of_block(pl.ds(pl.multiple_of(part * i, 16), part), ctx_ref, mid_ref, proj_ref, g2_ref, b2_ref,
                      fc1_ref, fc2_ref)
        return carry

    lax.fori_loop(0, 3, rest, 0)

    def side_copy(i, side):
        return pltpu.make_async_copy(
            own_ref.at[side, pl.ds(WLAT * i, WLAT)],
            out_hbm.at[pl.ds(SLAT + WLAT * i, WLAT), pl.ds(side * (cols - SLON), SLON)], out_sem.at[2 * i + side])

    def store(i, carry):
        at = pl.multiple_of(big * i, big)
        for side in range(2):
            block = from_level(take_levels(mid_ref, at + WIN * side, HALF), (WLAT, SLON, LEV, C))
            own_ref[side, pl.ds(WLAT * i, WLAT)] = block
            side_copy(i, side).start()
        return carry

    lax.fori_loop(0, steps, store, 0)
    outs = []
    for which in range(2):
        at = big * (steps + which)
        strip_ref[which, :, SLON : SLON + WLON] = from_level(take_levels(mid_ref, at, HALF), (SLAT, WLON, LEV, C))
        block = from_level(take_levels(mid_ref, at + WIN, HALF), (SLAT, WLON, LEV, C))
        strip_ref[which, :, cols - SLON :] = block[:, :SLON]
        strip_ref[which, :, :SLON] = block[:, SLON:]
        outs.append(pltpu.make_async_copy(strip_ref.at[which], out_hbm.at[strip_at[which]],
                                          out_sem.at[2 * steps + which]))
        outs[-1].start()
    for i in range(steps):
        for side in range(2):
            side_copy(i, side).wait()
    for copy in outs:
        copy.wait()


def passed_along(block, axis, distance):
    size = lax.axis_size(axis)
    return lax.ppermute(block, axis, [((i - distance) % size, i) for i in range(size)])


def per_device(tokens, norm1_gain, norm1_bias, qkv_weight, rel_bias, key_mask, proj_weight,
               norm2_gain, norm2_bias, fc1_weight, fc2_weight):
    rows, cols = tokens.shape[:2]
    north = passed_along(tokens[rows - SLAT :], "lat", 1)
    south = passed_along(tokens[:SLAT], "lat", -1)
    west = passed_along(tokens[:, cols - SLON :], "lon", 1)
    east = passed_along(tokens[:, :SLON], "lon", -1)

    vmem = pl.BlockSpec(memory_space=pltpu.VMEM)
    any_space = pl.BlockSpec(memory_space=pl.ANY)
    params = pltpu.CompilerParams(vmem_limit_bytes=VMEM_LIMIT)
    shape = (*key_mask.shape, rows, cols)
    bias1, bias2, valid = pl.pallas_call(
        functools.partial(prep_kernel, shape=shape),
        out_shape=[jax.ShapeDtypeStruct((HEADS, WIN, WIN), F32)] * 2 + [jax.ShapeDtypeStruct((21, 1, WIN), F32)],
        in_specs=[vmem, vmem],
        out_specs=[vmem] * 3,
        scratch_shapes=[pltpu.VMEM((HEADS, 768), F32), pltpu.VMEM((8 * WIN, 384), F32)],
        compiler_params=pltpu.CompilerParams(vmem_limit_bytes=40 * 1024 * 1024),
        cost_estimate=pl.CostEstimate(flops=10**9, bytes_accessed=5 * 10**6, transcendentals=0),
        name="prep",
    )(rel_bias, key_mask)

    def ends(at):
        return jnp.concatenate([north[:, at], south[:, at]], axis=0)

    west_ends = passed_along(ends(slice(cols - SLON, cols)), "lon", 1)
    east_ends = passed_along(ends(slice(0, SLON)), "lon", -1)

    g1, b1 = norm1_gain.reshape(1, C), norm1_bias.reshape(1, C)
    g2, b2 = norm2_gain.reshape(1, C), norm2_bias.reshape(1, C)
    count = 2 * WIN * ((rows - WLAT) // WLAT)
    weights = [pltpu.VMEM((C, C), BF), pltpu.VMEM((C, FF), BF), pltpu.VMEM((FF, C), BF)]
    table_shape = pltpu.VMEM((HEADS, WIN, WIN), F32)
    inner_shape = pltpu.VMEM((rows - 2 * SLAT, WLON, LEV, C), BF)
    part = pl.pallas_call(
        inner_kernel,
        out_shape=jax.ShapeDtypeStruct(tokens.shape, BF),
        in_specs=[any_space] * 6 + [vmem] * 5,
        out_specs=any_space,
        scratch_shapes=[inner_shape, pltpu.VMEM((C, 3 * C), BF), table_shape, *weights, inner_shape,
                        pltpu.VMEM((count, C), F32), pltpu.VMEM((count, C), F32),
                        pltpu.VMEM((count, 2 * C), BF), pltpu.VMEM((count, C), BF),
                        pltpu.SemaphoreType.DMA((6,)), pltpu.SemaphoreType.DMA((count // (2 * WIN),))],
        compiler_params=params,
        cost_estimate=pl.CostEstimate(flops=12 * 10**9, bytes_accessed=12 * 10**6, transcendentals=0),
        name="inner",
    )(tokens, qkv_weight, bias1, proj_weight, fc1_weight, fc2_weight, g1, b1, valid, g2, b2)

    own = count + 4 * WIN
    strip = (SLAT, cols, LEV, C)
    halo = (rows + 2 * SLAT, SLON, LEV, C)
    return pl.pallas_call(
        edge_kernel,
        out_shape=jax.ShapeDtypeStruct(tokens.shape, BF),
        in_specs=[any_space] * 14 + [vmem] * 5,
        out_specs=any_space,
        scratch_shapes=[pltpu.VMEM((2, rows - 2 * SLAT, SLON, LEV, C), BF), pltpu.VMEM((2, *strip), BF),
                        pltpu.VMEM(halo, BF), pltpu.VMEM(halo, BF), pltpu.VMEM(strip, BF), pltpu.VMEM(strip, BF),
                        pltpu.VMEM((C, 3 * C), BF), table_shape, table_shape, *weights,
                        pltpu.VMEM((8 * WIN, C), F32), pltpu.VMEM((4 * WIN, C), F32), pltpu.VMEM((8 * WIN, 2 * C), BF),
                        pltpu.VMEM((own, C), BF), pltpu.VMEM((own, C), F32),
                        pltpu.SemaphoreType.DMA((18,)), pltpu.SemaphoreType.DMA((own // WIN,))],
        input_output_aliases={0: 0},
        compiler_params=params,
        cost_estimate=pl.CostEstimate(flops=16 * 10**9, bytes_accessed=16 * 10**6, transcendentals=0),
        name="edge",
    )(part, tokens, west, east, north, south, west_ends, east_ends, qkv_weight, bias1, bias2, proj_weight, fc1_weight, fc2_weight,
      g1, b1, valid, g2, b2)


def solution(mesh):
    return jax.shard_map(
        per_device,
        mesh=mesh,
        in_specs=(P("lat", "lon", None, None),) + (P(),) * 10,
        out_specs=P("lat", "lon", None, None),
        check_vma=False,
    )
```

```python
import functools
import math

import jax
import jax.numpy as jnp
import numpy as np
from jax import lax
from jax.experimental import pallas as pl
from jax.experimental.pallas import tpu as pltpu
from jax.sharding import PartitionSpec as P

C = 512
FF = 2048
HEADS = 8
HEAD_DIM = 64
WLEV = 2
WLAT = 6
WLON = 12
LEV = 4
SLAT = 3
SLON = 6
WIN = WLAT * WLON * WLEV
HALF = WIN // 2
QUART = WIN // 4
EPS = 1e-5
LOG2E = math.log2(math.e)
NEG = -jnp.inf
BF = jnp.bfloat16
F32 = jnp.float32
PAIRS = ((1, 2), (3, 0))
VMEM_LIMIT = 44 * 1024 * 1024


def order_columns():
    first = [(p, 6 * h + q, r) for h in range(2) for r in range(2) for p in range(6) for q in range(6)]
    second = [(3 * h + p, q, r) for h in range(2) for r in range(2) for p in range(3) for q in range(12)]
    return first, second


def lane_pqr(u, which):
    half, r, cell = u // HALF, (u // QUART) % 2, u % QUART
    if which == 0:
        return cell // 6, 6 * half + cell % 6, r
    return 3 * half + cell // 12, cell % 12, r


def prep_kernel(table_ref, mask_ref, bias1_ref, bias2_ref, valid_ref, wide_ref, rows_ref, *, shape):
    nlat, nlon, tile_rows, tile_cols = shape
    lat, lon, lats = lax.axis_index("lat"), lax.axis_index("lon"), nlat // tile_rows
    first, second = order_columns()
    wide_ref[...] = jnp.zeros_like(wide_ref)
    wide_ref[:, : table_ref.shape[1]] = table_ref[...] * LOG2E
    for t, (p, q, r) in enumerate(first):
        start = p * 69 + q * 3 + r
        rows_ref[8 * t : 8 * t + 8, :] = wide_ref[:, start : start + 384]
    rows = rows_ref[...]
    high = rows.astype(BF)
    low = (rows - high.astype(F32)).astype(BF)
    k = lax.broadcasted_iota(jnp.int32, (384, WIN), 0)
    for which, out_ref in enumerate((bias1_ref, bias2_ref)):
        p, q, r = lane_pqr(lax.broadcasted_iota(jnp.int32, (1, WIN), 1), which)
        pick = jnp.where(k == 379 - (p * 69 + q * 3 + r), 1.0, 0.0).astype(BF)
        full = jnp.dot(high, pick, preferred_element_type=F32) + jnp.dot(low, pick, preferred_element_type=F32)
        full = full.reshape(WIN, HEADS, WIN)
        if which == 1:
            full = jnp.stack([full[first.index(pqr)] for pqr in second])
        out_ref[...] = jnp.transpose(full, (1, 0, 2))
    row = lax.broadcasted_iota(jnp.int32, (48, 1), 0)
    col = lax.broadcasted_iota(jnp.int32, (48, nlat), 1)
    want = lax.rem(lat * tile_rows - SLAT + row + nlat, nlat)
    pick_rows = jnp.where(want == col, 1.0, 0.0).astype(BF)
    mask = (mask_ref[...] > 0).astype(F32).astype(BF)
    picked = jnp.dot(pick_rows, mask, preferred_element_type=F32).astype(BF)
    row = lax.broadcasted_iota(jnp.int32, (nlon, 3 * WIN), 0)
    row48 = lax.broadcasted_iota(jnp.int32, (48, 3 * WIN), 0)
    lane = lax.broadcasted_iota(jnp.int32, (1, 3 * WIN), 1)
    for which in range(2):
        p, q, _ = lane_pqr(lane % WIN, which)
        want = lax.rem(lon * tile_cols - SLON + 12 * (lane // WIN) + q + nlon, nlon)
        pick_cols = jnp.where(want == row, 1.0, 0.0).astype(BF)
        spread = jnp.dot(picked, pick_cols, preferred_element_type=F32)
        for window in (range(1, 6) if which == 0 else (0, 6)):
            value = jnp.sum(jnp.where(row48 == 6 * window + p, spread, 0.0), axis=0, keepdims=True)
            ok = value > 0.5
            if window == 0:
                ok = ok & ((lat > 0) | (lane % WIN >= HALF))
            if window == 6:
                ok = ok & ((lat < lats - 1) | (lane % WIN < HALF))
            value = jnp.where(ok, 0.0, NEG)
            for n in range(3):
                valid_ref[3 * window + n] = value[:, n * WIN : (n + 1) * WIN]


def layer_norm(values, gain, offset):
    average = jnp.mean(values, axis=-1, keepdims=True)
    centred = values - average
    spread = jnp.mean(centred * centred, axis=-1, keepdims=True)
    return centred * lax.rsqrt(spread + EPS) * gain + offset


def by_level(block):
    cells = block.astype(F32).reshape(QUART, LEV, C)
    return jnp.transpose(cells, (1, 0, 2))


def from_level(rows, shape):
    return jnp.transpose(rows, (1, 0, 2)).reshape(shape).astype(BF)


def attend(q, k, v, bias_of, block_mask):
    n = q.shape[0]
    head_of = lax.broadcasted_iota(jnp.int32, (1, 2 * HEAD_DIM), 1) // HEAD_DIM
    ones = jnp.ones((WIN, 2 * HEAD_DIM), BF)
    parts = []
    for g in range(HEADS // 2):
        lanes = slice(2 * HEAD_DIM * g, 2 * HEAD_DIM * (g + 1))
        qg = q[:, lanes]
        stacked = jnp.concatenate([jnp.where(head_of == j, qg, 0.0) for j in range(2)], axis=0).astype(BF)
        scores = lax.dot_general(stacked, k[:, lanes], (((1,), (1,)), ((), ())), preferred_element_type=F32)
        probs = []
        for j in range(2):
            s = scores[j * n : (j + 1) * n] + (bias_of(2 * g + j) + block_mask)
            probs.append(jnp.exp2(s - jnp.max(s, axis=-1, keepdims=True)))
        probs = jnp.concatenate(probs, axis=0).astype(BF)
        out = jnp.dot(probs, jnp.concatenate([v[:, lanes], ones], axis=1), preferred_element_type=F32)
        out = jnp.where(jnp.concatenate([head_of, head_of], axis=1) == 0, out[:n], out[n:])
        parts.append(out[:, : 2 * HEAD_DIM] / out[:, 2 * HEAD_DIM :])
    return jnp.concatenate(parts, axis=1)


def feed(middle, gain, offset, fc1_ref, fc2_ref):
    normed = jnp.concatenate([layer_norm(middle[at : at + 48], gain, offset).astype(BF)
                              for at in range(0, middle.shape[0], 48)], axis=0)
    total = None
    for j in range(4):
        v = jnp.dot(normed, fc1_ref[:, 512 * j : 512 * j + 512], preferred_element_type=F32)
        hidden = (v + v * lax.erf(v * (0.5 ** 0.5))).astype(BF)
        part = jnp.dot(hidden, fc2_ref[512 * j : 512 * j + 512, :], preferred_element_type=F32)
        total = part if total is None else total + part
    return middle + 0.5 * total


def block_masks(valid, first, n):
    t = lax.broadcasted_iota(jnp.int32, (n, 1), 0) + first
    u = lax.broadcasted_iota(jnp.int32, (1, WIN), 1)
    joint = jnp.where(t == u, 0.0, jnp.broadcast_to(valid, (n, WIN)))
    same = (t // QUART) % 2 == (u // QUART) % 2
    return joint, jnp.where(same, joint, NEG)


def put_block(block, gain, offset, normed_to=(), raw_to=()):
    levels = by_level(block)
    for pair in range(2):
        rows = jnp.concatenate([levels[level] for level in PAIRS[pair]], axis=0)
        normed = layer_norm(rows, gain, offset)
        for places, value in ((raw_to, rows), (normed_to, normed)):
            for ref, at, step in places:
                ref[pl.ds(pl.multiple_of(at + step * pair, 8), HALF), :] = value


def take_levels(from_ref, at, step):
    levels = [None] * LEV
    for pair in range(2):
        rows = from_ref[pl.ds(pl.multiple_of(at + step * pair, 8), HALF), :]
        for r in range(2):
            levels[PAIRS[pair][r]] = rows[QUART * r : QUART * r + QUART]
    return jnp.stack(levels)


def rest_of_block(rows, ctx_ref, xs_ref, proj_ref, g2_ref, b2_ref, fc1_ref, fc2_ref):
    moved = jnp.dot(ctx_ref[rows, :], proj_ref[...], preferred_element_type=F32).astype(BF)
    middle = xs_ref[rows, :] + moved.astype(F32)
    xs_ref[rows, :] = feed(middle, g2_ref[...], b2_ref[...], fc1_ref, fc2_ref)


def start_copies(pairs, sem):
    copies = [pltpu.make_async_copy(src, dst, sem.at[n]) for n, (src, dst) in enumerate(pairs)]
    for copy in copies:
        copy.start()
    return copies


Q_SCALE = HEAD_DIM ** -0.5 * LOG2E


def inner_kernel(tok_hbm, qkv_hbm, bias_hbm, proj_hbm, fc1_hbm, fc2_hbm, g1_ref, b1_ref, valid_ref, g2_ref, b2_ref,
                 out_hbm, tok_ref, qkv_ref, bias_ref, proj_ref, fc1_ref, fc2_ref, out_ref, xs_ref, q_ref,
                 kv_ref, ctx_ref, sem, out_sem):
    steps = tok_ref.shape[0] // WLAT
    inner = (pl.ds(SLAT, WLAT * steps), pl.ds(SLON, WLON))
    copies = start_copies([(tok_hbm.at[inner], tok_ref), (qkv_hbm, qkv_ref), (bias_hbm, bias_ref),
                           (proj_hbm, proj_ref), (fc1_hbm, fc1_ref), (fc2_hbm, fc2_ref)], sem)
    big = 2 * WIN
    part = big * steps // 2

    copies[0].wait()

    def load(i):
        at = pl.multiple_of(big * i, big)
        x = tok_ref[pl.ds(WLAT * i, WLAT)]
        for h in range(2):
            put_block(x[:, 6 * h : 6 * h + 6], g1_ref[...], b1_ref[...], [(q_ref, at + HALF * h, WIN)],
                      [(xs_ref, at + HALF * h, WIN)])

    for i in range(steps):
        load(i)
    copies[1].wait()

    def project(i, carry):
        rows = pl.ds(pl.multiple_of(part * i, 16), part)
        normed = q_ref[rows, :].astype(BF)
        q_ref[rows, :] = jnp.dot(normed, qkv_ref[:, :C], preferred_element_type=F32) * Q_SCALE
        kv_ref[rows, :] = jnp.dot(normed, qkv_ref[:, C:], preferred_element_type=F32).astype(BF)
        return carry

    lax.fori_loop(0, 2, project, 0)
    copies[2].wait()

    def attention(i):
        masks = block_masks(valid_ref[3 * (i + 1) + 1], 0, WIN)
        for pair in range(2):
            rows = pl.ds(pl.multiple_of(big * i + WIN * pair, WIN), WIN)
            ctx_ref[rows, :] = attend(q_ref[rows, :], kv_ref[rows, :C], kv_ref[rows, C:],
                                      lambda h: bias_ref[h], masks[pair]).astype(BF)

    for i in range(steps):
        attention(i)
    for copy in copies[3:]:
        copy.wait()

    def rest(i, carry):
        rest_of_block(pl.ds(pl.multiple_of(part * i, 16), part), ctx_ref, xs_ref, proj_ref, g2_ref, b2_ref,
                      fc1_ref, fc2_ref)
        return carry

    lax.fori_loop(0, 2, rest, 0)

    def out_copy(i):
        return pltpu.make_async_copy(out_ref.at[pl.ds(WLAT * i, WLAT)],
                                     out_hbm.at[pl.ds(SLAT + WLAT * i, WLAT), pl.ds(SLON, WLON)], out_sem.at[i])

    def store(i, carry):
        for h in range(2):
            levels = take_levels(xs_ref, pl.multiple_of(big * i, big) + HALF * h, WIN)
            out_ref[pl.ds(WLAT * i, WLAT), 6 * h : 6 * h + 6] = from_level(levels, (WLAT, 6, LEV, C))
        out_copy(i).start()
        return carry

    lax.fori_loop(0, steps, store, 0)
    for i in range(steps):
        out_copy(i).wait()


def edge_kernel(part_hbm, tok_hbm, west_hbm, east_hbm, north_hbm, south_hbm, nw_hbm, sw_hbm, ne_hbm, se_hbm, qkv_hbm, bias1_hbm, bias2_hbm, proj_hbm,
                fc1_hbm, fc2_hbm, g1_ref, b1_ref, valid_ref, g2_ref, b2_ref, out_hbm,
                own_ref, strip_ref, west_ref, east_ref, north_ref, south_ref, qkv_ref, bias1_ref, bias2_ref, proj_ref,
                fc1_ref, fc2_ref, xs_ref, q_ref, kv_ref, ctx_ref, mid_ref, sem, out_sem):
    del part_hbm
    rows, cols = tok_hbm.shape[:2]
    steps = (rows - WLAT) // WLAT
    side_at = ((pl.ds(SLAT, WLAT * steps), pl.ds(0, SLON)), (pl.ds(SLAT, WLAT * steps), pl.ds(cols - SLON, SLON)))
    strip_at = (pl.ds(0, SLAT), pl.ds(rows - SLAT, SLAT))
    places = [(own_ref.at[side], side_at[side]) for side in range(2)]
    places += [(strip_ref.at[which], strip_at[which]) for which in range(2)]
    copies = start_copies([(tok_hbm.at[at], here) for here, at in places[:2]] + [
        (west_hbm, west_ref.at[pl.ds(SLAT, rows)]), (east_hbm, east_ref.at[pl.ds(SLAT, rows)]), (qkv_hbm, qkv_ref), (bias1_hbm, bias1_ref)] + [
        (tok_hbm.at[at], here) for here, at in places[2:]] + [
        (nw_hbm, west_ref.at[pl.ds(0, SLAT)]), (sw_hbm, west_ref.at[pl.ds(rows + SLAT, SLAT)]),
        (ne_hbm, east_ref.at[pl.ds(0, SLAT)]), (se_hbm, east_ref.at[pl.ds(rows + SLAT, SLAT)]),
        (north_hbm, north_ref), (south_hbm, south_ref), (bias2_hbm, bias2_ref), (proj_hbm, proj_ref),
        (fc1_hbm, fc1_ref), (fc2_hbm, fc2_ref)], sem)
    big = 2 * WIN

    for copy in copies[:6]:
        copy.wait()

    def sides(i):
        at = big * i
        base, mine_base = 2 * big * (i % 2), big * (i % 2)
        own_rows, halo_rows = pl.ds(WLAT * i, WLAT), pl.ds(2 * SLAT + WLAT * i, WLAT)
        for side, halo_ref in ((0, west_ref), (1, east_ref)):
            here, there = (HALF, 0) if side == 0 else (0, HALF)
            put_block(own_ref[side, own_rows], g1_ref[...], b1_ref[...],
                      [(xs_ref, base + big * side + here, WIN)], [(mid_ref, at + WIN * side, HALF)])
            put_block(halo_ref[halo_rows], g1_ref[...], b1_ref[...], [(xs_ref, base + big * side + there, WIN)])
        keys_all = slice(base, base + 2 * big)
        kv_ref[keys_all, :] = jnp.dot(xs_ref[keys_all, :].astype(BF), qkv_ref[:, C:],
                                      preferred_element_type=F32).astype(BF)
        own = jnp.concatenate([xs_ref[base + row : base + row + HALF, :]
                               for row in (HALF, WIN + HALF, big, big + WIN)], axis=0)
        q_ref[mine_base : mine_base + big, :] = jnp.dot(own.astype(BF), qkv_ref[:, :C],
                                                        preferred_element_type=F32) * Q_SCALE
        contexts = []
        for side in range(2):
            first = HALF if side == 0 else 0
            masks = block_masks(valid_ref[3 * (i + 1) + 2 * side], first, HALF)
            for pair in range(2):
                mine, keys = mine_base + WIN * side + HALF * pair, base + big * side + WIN * pair
                contexts.append(attend(q_ref[mine : mine + HALF, :], kv_ref[keys : keys + WIN, :C],
                                       kv_ref[keys : keys + WIN, C:],
                                       lambda h: bias1_ref[h, first : first + HALF, :], masks[pair]))
        ctx_ref[at : at + big, :] = jnp.concatenate(contexts, axis=0).astype(BF)

    for i in range(steps):
        sides(i)
    for copy in copies[6:15]:
        copy.wait()

    for which in range(2):
        at = big * (steps + which)
        first = HALF if which == 0 else 0
        inside = slice(SLAT, 2 * SLAT) if which == 0 else slice(rows, rows + SLAT)
        outside = slice(0, SLAT) if which == 0 else slice(rows + SLAT, rows + 2 * SLAT)
        near_ref = (north_ref, south_ref)[which]
        own = jnp.concatenate([west_ref[inside], strip_ref[which], east_ref[inside]], axis=1)
        halo = jnp.concatenate([west_ref[outside], near_ref[...], east_ref[outside]], axis=1)
        for k in range(3):
            window = slice(WLON * k, WLON * k + WLON)
            mid = k == 1
            put_block(own[:, window], g1_ref[...], b1_ref[...],
                      [(xs_ref, big * k + first, WIN)] + ([(q_ref, 0, HALF)] if mid else []),
                      [(mid_ref, at, HALF)] if mid else [])
            put_block(halo[:, window], g1_ref[...], b1_ref[...], [(xs_ref, big * k + HALF - first, WIN)])
        corner = jnp.concatenate([strip_ref[which, :, cols - SLON :], strip_ref[which, :, :SLON]], axis=1)
        put_block(corner, g1_ref[...], b1_ref[...], [(q_ref, WIN, HALF)], [(mid_ref, at + WIN, HALF)])
        kv_ref[: 3 * big, :] = jnp.dot(xs_ref[: 3 * big, :].astype(BF), qkv_ref[:, C:],
                                       preferred_element_type=F32).astype(BF)
        q_ref[:big, :] = jnp.dot(q_ref[:big, :].astype(BF), qkv_ref[:, :C], preferred_element_type=F32) * Q_SCALE
        contexts = {}
        for k in range(3):
            masks = block_masks(valid_ref[18 * which + k], first, HALF)
            for pair in range(2):
                mine, keys = (0 if k == 1 else WIN) + HALF * pair, big * k + WIN * pair
                contexts[k, pair] = attend(q_ref[mine : mine + HALF, :], kv_ref[keys : keys + WIN, :C],
                                           kv_ref[keys : keys + WIN, C:],
                                           lambda h: bias2_ref[h, first : first + HALF, :], masks[pair])
        east_cell = lax.broadcasted_iota(jnp.int32, (HALF, 1), 0) % WLON < SLON
        ctx_ref[at : at + big, :] = jnp.concatenate(
            [contexts[1, 0], contexts[1, 1]] + [jnp.where(east_cell, contexts[2, pair], contexts[0, pair])
                                                for pair in range(2)], axis=0).astype(BF)
    for copy in copies[15:]:
        copy.wait()
    part = big * (steps + 2) // 3

    def rest(i, carry):
        rest_of_block(pl.ds(pl.multiple_of(part * i, 16), part), ctx_ref, mid_ref, proj_ref, g2_ref, b2_ref,
                      fc1_ref, fc2_ref)
        return carry

    lax.fori_loop(0, 3, rest, 0)

    def side_copy(i, side):
        return pltpu.make_async_copy(
            own_ref.at[side, pl.ds(WLAT * i, WLAT)],
            out_hbm.at[pl.ds(SLAT + WLAT * i, WLAT), pl.ds(side * (cols - SLON), SLON)], out_sem.at[2 * i + side])

    def store(i, carry):
        at = pl.multiple_of(big * i, big)
        for side in range(2):
            block = from_level(take_levels(mid_ref, at + WIN * side, HALF), (WLAT, SLON, LEV, C))
            own_ref[side, pl.ds(WLAT * i, WLAT)] = block
            side_copy(i, side).start()
        return carry

    lax.fori_loop(0, steps, store, 0)
    outs = []
    for which in range(2):
        at = big * (steps + which)
        strip_ref[which, :, SLON : SLON + WLON] = from_level(take_levels(mid_ref, at, HALF), (SLAT, WLON, LEV, C))
        block = from_level(take_levels(mid_ref, at + WIN, HALF), (SLAT, WLON, LEV, C))
        strip_ref[which, :, cols - SLON :] = block[:, :SLON]
        strip_ref[which, :, :SLON] = block[:, SLON:]
        outs.append(pltpu.make_async_copy(strip_ref.at[which], out_hbm.at[strip_at[which]],
                                          out_sem.at[2 * steps + which]))
        outs[-1].start()
    for i in range(steps):
        for side in range(2):
            side_copy(i, side).wait()
    for copy in outs:
        copy.wait()


def passed_along(block, axes, distance):
    sizes = [lax.axis_size(a) for a in axes]
    route = []
    for i in np.ndindex(*sizes):
        j = tuple((a - d) % n for a, d, n in zip(i, distance, sizes))
        route.append((int(np.ravel_multi_index(j, sizes)), int(np.ravel_multi_index(i, sizes))))
    return lax.ppermute(block, axes if len(axes) > 1 else axes[0], route)


def per_device(tokens, norm1_gain, norm1_bias, qkv_weight, rel_bias, key_mask, proj_weight,
               norm2_gain, norm2_bias, fc1_weight, fc2_weight):
    rows, cols = tokens.shape[:2]
    first, last = slice(0, SLAT), slice(rows - SLAT, rows)
    left, right = slice(0, SLON), slice(cols - SLON, cols)
    north = passed_along(tokens[last], ("lat",), (1,))
    south = passed_along(tokens[first], ("lat",), (-1,))
    west = passed_along(tokens[:, right], ("lon",), (1,))
    east = passed_along(tokens[:, left], ("lon",), (-1,))
    both = ("lon", "lat")
    nw = passed_along(tokens[last, right], both, (1, 1))
    sw = passed_along(tokens[first, right], both, (1, -1))
    ne = passed_along(tokens[last, left], both, (-1, 1))
    se = passed_along(tokens[first, left], both, (-1, -1))

    vmem = pl.BlockSpec(memory_space=pltpu.VMEM)
    any_space = pl.BlockSpec(memory_space=pl.ANY)
    params = pltpu.CompilerParams(vmem_limit_bytes=VMEM_LIMIT)
    shape = (*key_mask.shape, rows, cols)
    bias1, bias2, valid = pl.pallas_call(
        functools.partial(prep_kernel, shape=shape),
        out_shape=[jax.ShapeDtypeStruct((HEADS, WIN, WIN), F32)] * 2 + [jax.ShapeDtypeStruct((21, 1, WIN), F32)],
        in_specs=[vmem, vmem],
        out_specs=[vmem] * 3,
        scratch_shapes=[pltpu.VMEM((HEADS, 768), F32), pltpu.VMEM((8 * WIN, 384), F32)],
        compiler_params=pltpu.CompilerParams(vmem_limit_bytes=40 * 1024 * 1024),
        cost_estimate=pl.CostEstimate(flops=10**9, bytes_accessed=5 * 10**6, transcendentals=0),
        name="prep",
    )(rel_bias, key_mask)

    g1, b1 = norm1_gain.reshape(1, C), norm1_bias.reshape(1, C)
    g2, b2 = norm2_gain.reshape(1, C), norm2_bias.reshape(1, C)
    count = 2 * WIN * ((rows - WLAT) // WLAT)
    weights = [pltpu.VMEM((C, C), BF), pltpu.VMEM((C, FF), BF), pltpu.VMEM((FF, C), BF)]
    table_shape = pltpu.VMEM((HEADS, WIN, WIN), F32)
    inner_shape = pltpu.VMEM((rows - 2 * SLAT, WLON, LEV, C), BF)
    part = pl.pallas_call(
        inner_kernel,
        out_shape=jax.ShapeDtypeStruct(tokens.shape, BF),
        in_specs=[any_space] * 6 + [vmem] * 5,
        out_specs=any_space,
        scratch_shapes=[inner_shape, pltpu.VMEM((C, 3 * C), BF), table_shape, *weights, inner_shape,
                        pltpu.VMEM((count, C), F32), pltpu.VMEM((count, C), F32),
                        pltpu.VMEM((count, 2 * C), BF), pltpu.VMEM((count, C), BF),
                        pltpu.SemaphoreType.DMA((6,)), pltpu.SemaphoreType.DMA((count // (2 * WIN),))],
        compiler_params=params,
        cost_estimate=pl.CostEstimate(flops=12 * 10**9, bytes_accessed=12 * 10**6, transcendentals=0),
        name="inner",
    )(tokens, qkv_weight, bias1, proj_weight, fc1_weight, fc2_weight, g1, b1, valid, g2, b2)

    own = count + 4 * WIN
    strip = (SLAT, cols, LEV, C)
    halo = (rows + 2 * SLAT, SLON, LEV, C)
    return pl.pallas_call(
        edge_kernel,
        out_shape=jax.ShapeDtypeStruct(tokens.shape, BF),
        in_specs=[any_space] * 16 + [vmem] * 5,
        out_specs=any_space,
        scratch_shapes=[pltpu.VMEM((2, rows - 2 * SLAT, SLON, LEV, C), BF), pltpu.VMEM((2, *strip), BF),
                        pltpu.VMEM(halo, BF), pltpu.VMEM(halo, BF), pltpu.VMEM(strip, BF), pltpu.VMEM(strip, BF),
                        pltpu.VMEM((C, 3 * C), BF), table_shape, table_shape, *weights,
                        pltpu.VMEM((8 * WIN, C), F32), pltpu.VMEM((4 * WIN, C), F32), pltpu.VMEM((8 * WIN, 2 * C), BF),
                        pltpu.VMEM((own, C), BF), pltpu.VMEM((own, C), F32),
                        pltpu.SemaphoreType.DMA((18,)), pltpu.SemaphoreType.DMA((own // WIN,))],
        input_output_aliases={0: 0},
        compiler_params=params,
        cost_estimate=pl.CostEstimate(flops=16 * 10**9, bytes_accessed=16 * 10**6, transcendentals=0),
        name="edge",
    )(part, tokens, west, east, north, south, nw, sw, ne, se, qkv_weight, bias1, bias2, proj_weight, fc1_weight, fc2_weight,
      g1, b1, valid, g2, b2)


def solution(mesh):
    return jax.shard_map(
        per_device,
        mesh=mesh,
        in_specs=(P("lat", "lon", None, None),) + (P(),) * 10,
        out_specs=P("lat", "lon", None, None),
        check_vma=False,
    )
```
